32 devices in a mesh: ind: 8 (over z, x), snp: 4 (over y, core).
Axes of the slice: x: 2, y: 2, z: 4, core: 2. Of those that a mesh axis runs over, the one named last changes fastest.
Arguments:
- genotype: int32 [4096, 8192], P('ind', 'snp'), may hold values from 0 to 170, as said below
- probe: bfloat16 [24, 8192], P(None, 'snp'), may hold values from -0.0625 to 0.0625
- allele_mean: float32 [8192], P('snp'), may hold values from 0.2 to 1.8
- allele_scale: float32 [8192], P('snp'), may hold values from 0.3 to 3
Outputs:
- projected: float32 [24, 8192], P(None, 'snp')
The draws below stay inside these ranges and needn't reach their ends.
Inputs may be any that keep to these rules, and one draw needn't show every extreme that they name: `genotype`: word r of a column holds the codes of individuals 4 r + k, k = 0 to 3, in bits 2 k and 2 k + 1; every code is 0, 1 or 2.
All inputs are finite; a program needn't handle non-finite values.
Results may differ from the reference program's by a relative error of at most 0.0095.
Values may be sent and summed in bfloat16 or wider, within the bound.
A program may use at most 64 MiB of HBM per device.

```python
import math
import jax
import jax.numpy as jnp
from jax import lax

RANK = 24
NIND = 16384
NSNP = 8192


def draw_genotype(key, part):
    key_anc, key_cut, key_codes = jax.random.split(key, 3)
    ancestry = jax.random.randint(key_anc, (4, NIND // 4), 0, 4)
    thresholds = jax.random.randint(key_cut, (4, NSNP), 2, 15)
    packed = jnp.zeros((NIND // 4, NSNP), jnp.int32)
    for offset in range(4):
        key_plane = jax.random.fold_in(key_codes, offset)
        key_first, key_second = jax.random.split(key_plane)
        cutoff = thresholds[ancestry[offset]]
        first_draw = jax.random.randint(key_first, (NIND // 4, NSNP), 0, 16)
        second_draw = jax.random.randint(key_second, (NIND // 4, NSNP), 0, 16)
        codes = (first_draw < cutoff).astype(jnp.int32) + (second_draw < cutoff).astype(jnp.int32)
        packed = jnp.bitwise_or(packed, jnp.left_shift(codes, 2 * offset))
    packed = packed.at[0, 0].set(jnp.array(170, jnp.int32))
    packed = packed.at[0, 1].set(jnp.array(0, jnp.int32))
    return packed


def shard_levels(stream_key, shape, cuts, smallest, high):
    def one(position, blocks):
        steps = jax.random.uniform(jax.random.fold_in(jax.random.fold_in(stream_key, 6), position), (blocks,), jnp.float32, smallest / len(cuts), high / len(cuts))
        return jnp.repeat(jnp.exp(steps), shape[position] // blocks).reshape((-1,) + (1,) * (len(shape) - position - 1))

    loudness = one(*cuts[0])
    for cut in cuts[1:]:
        loudness = loudness * one(*cut)
    return loudness


def gaussian(rng, extent, deviation, bound, shards=(), dtype=jnp.bfloat16):
    drawn = jax.random.normal(rng, extent, jnp.float32) * deviation
    if len(shards) > 0:
        drawn = shard_levels(rng, extent, shards, -0.22, 0.18) * drawn
    return jnp.clip(drawn, min=-bound, max=bound).astype(dtype)


def setup_inputs(seed: int = 0) -> dict:
    arg_keys = jax.random.split(jax.random.key(seed), 5)
    return {
        "genotype": draw_genotype(jax.random.fold_in(arg_keys[4], 71), 0),
        "probe": gaussian(arg_keys[1], (RANK, NSNP), NSNP ** -0.5, 0.0625, ((1, 4),)),
        "allele_mean": jnp.clip(0.2 + 1.5999999 * jax.random.uniform(arg_keys[2], (NSNP,), jnp.float32) ** shard_levels(arg_keys[2], (NSNP,), ((0, 4),), -0.2, 0.2), 0.2, 1.8),
        "allele_scale": jnp.clip(jnp.exp(math.log(3.0) - 2.3025851 * jax.random.uniform(arg_keys[3], (NSNP,), jnp.float32) ** shard_levels(arg_keys[3], (NSNP,), ((0, 4),), -0.2, 0.2)), 0.3, 3.0),
    }


def unpack(packed, allele_mean, allele_scale):
    planes = []
    for offset in range(4):
        codes = jnp.bitwise_and(jnp.right_shift(packed, 2 * offset), 3)
        planes.append(((codes.astype(jnp.float32) - allele_mean) * allele_scale).astype(jnp.bfloat16))
    stacked = jnp.stack(planes, axis=1)
    return stacked.reshape(packed.shape[0] * 4, packed.shape[1])

def reference(genotype, probe, allele_mean, allele_scale):
    block_rows = math.gcd(NIND // 4, 32)
    block_count = NIND // 4 // block_rows
    packed_blocks = genotype.reshape(block_count, block_rows, NSNP)

    def sketch_step(carry, packed):
        zed = unpack(packed, allele_mean, allele_scale)
        return (carry, jnp.dot(zed.astype(jnp.float32), probe.T.astype(jnp.float32), preferred_element_type=jnp.float32))
    ignored, pieces = lax.scan(sketch_step, jnp.zeros((), jnp.float32), packed_blocks)
    sketch = pieces.reshape(NIND, RANK).T
    gram = jnp.dot(sketch.astype(jnp.float32), sketch.T.astype(jnp.float32), precision=lax.Precision.HIGHEST, preferred_element_type=jnp.float32)
    lower = jnp.linalg.cholesky(gram)
    basis = jax.scipy.linalg.solve_triangular(lower, sketch, lower=True).astype(jnp.bfloat16)
    basis_blocks = basis.reshape(RANK, block_count, 4 * block_rows).transpose(1, 0, 2)

    def project_step(total, inputs):
        packed, basis_block = inputs
        zed = unpack(packed, allele_mean, allele_scale)
        return (total + jnp.dot(basis_block.astype(jnp.float32), zed.astype(jnp.float32), preferred_element_type=jnp.float32), 0.0)
    projected, ignored_too = lax.scan(project_step, jnp.zeros((RANK, NSNP), jnp.float32), (packed_blocks, basis_blocks))
    return projected
```

```python
import functools

import jax
import jax.numpy as jnp
from jax import lax
from jax.experimental import pallas as pl
from jax.experimental.pallas import tpu as pltpu
from jax.sharding import PartitionSpec as P

MESH = pl.DeviceIdType.MESH
CORES = 2
CHUNKS = 4
PLANES = 4


def fold(x):
    half = x.shape[1] // 2
    return jnp.concatenate([x[:, :half], x[:, half:]], axis=0)


def unfold(x):
    rows = x.shape[0] // 2
    return jnp.concatenate([x[:rows], x[rows:]], axis=1)


def dot_nt(a, b):
    return lax.dot_general(
        a, b, (((1,), (1,)), ((), ())), preferred_element_type=jnp.float32
    )


def inverse_factor(packed, rank):
    groups = rank // 8
    a = jnp.concatenate([packed[:, 32 * g : 32 * g + 32] for g in range(groups)], axis=0)
    shape = (rank, 128)
    row_id = lax.broadcasted_iota(jnp.int32, shape, 0)
    lane_id = lax.broadcasted_iota(jnp.int32, shape, 1)
    eye = jnp.where(lane_id == row_id + 32, 1.0, 0.0).astype(jnp.float32)
    m = jnp.concatenate([a, jnp.zeros((rank, 96), jnp.float32)], axis=1) + eye
    rows1 = lax.broadcasted_iota(jnp.int32, (rank, 1), 0)
    for p in range(rank - 1):
        factor = jnp.where(rows1 > p, m[:, p : p + 1] / m[p : p + 1, p : p + 1], 0.0)
        m = m - factor * m[p : p + 1, :]
    pivots = jnp.sum(jnp.where(lane_id == row_id, m, 0.0), axis=1, keepdims=True)
    return m[:, 32 : 32 + rank] * (1.0 / jnp.sqrt(pivots))


def kernel(
    n, ny, g_hbm, probe_ref, mean_ref, scale_ref, out_ref,
    words, codes, weights, means, scales, sk, rx_core, ry, s_out, s_in, s_cat,
    rg, qacc, rs_out, rs_in, ag,
    load_sem, core_send, core_recv, y_send, y_recv, s_send, s_recv,
    g_send, g_recv, rs_send, rs_recv, ag_send, ag_recv,
):
    rank, cols = probe_ref.shape
    w = cols // n
    half = words.shape[0] // 2
    cw = half // CHUNKS
    ci = cw * PLANES
    group = n * CORES
    ind = lax.axis_index("ind")
    snp = lax.axis_index("snp")
    core = lax.rem(snp, CORES)
    y = lax.div(snp, CORES)
    other = snp + 1 - 2 * core
    gme = ind * CORES + core

    def load(c):
        h, k = divmod(c, CHUNKS) if isinstance(c, int) else (lax.div(c, CHUNKS), lax.rem(c, CHUNKS))
        where = jnp.where(h == 0, 1 - core, core)
        row = pl.multiple_of(where * half + k * cw, 8)
        at = pl.multiple_of(c * cw, 8)
        return pltpu.make_async_copy(
            g_hbm.at[pl.ds(row, cw), :], words.at[pl.ds(at, cw), :], load_sem.at[c]
        )

    for c in range(2 * CHUNKS):
        load(c).start()

    barrier = pltpu.get_barrier_semaphore()

    def greet(k, carry):
        to = lax.rem(gme + k, group)
        pl.semaphore_signal(
            barrier, inc=1, device_id=(lax.div(to, CORES), y * CORES + lax.rem(to, CORES)),
            device_id_type=MESH,
        )
        return carry

    lax.fori_loop(1, group, greet, 0)
    for k in range(1, ny):
        pl.semaphore_signal(
            barrier, inc=1, device_id=(ind, lax.rem(y + k, ny) * CORES + core),
            device_id_type=MESH,
        )

    scale = scale_ref[...]
    mean = mean_ref[...]
    scaled = probe_ref[...].astype(jnp.float32) * scale
    const = jnp.sum(scaled * mean, axis=1, keepdims=True)
    high = scaled.astype(jnp.bfloat16).astype(jnp.float32)
    both = jnp.concatenate([high, scaled - high], axis=0).astype(jnp.bfloat16)
    for b in range(n):
        weights[b] = both[:, b * w : (b + 1) * w]
        means[b] = mean[:, b * w : (b + 1) * w]
        scales[b] = scale[:, b * w : (b + 1) * w]

    def sketch_chunk(c):
        load(c).wait()
        at = pl.multiple_of(c * cw, 8)
        total = jnp.zeros((2 * rank, ci), jnp.float32)
        for b in range(n):
            packed = words[pl.ds(at, cw), b * w : (b + 1) * w]
            for k in range(PLANES):
                plane = ((packed >> (2 * k)) & 3).astype(jnp.float32).astype(jnp.bfloat16)
                codes[b, pl.ds(pl.multiple_of(c * ci + k * cw, 16), cw), :] = plane
            total += dot_nt(weights[b], codes[b, pl.ds(pl.multiple_of(c * ci, 16), ci), :])
        return total[:rank] + total[rank:] - const

    def first(c, carry):
        sk[c] = sketch_chunk(c)
        return carry

    lax.fori_loop(0, CHUNKS, first, 0)
    pl.semaphore_wait(barrier, group - 1 + ny - 1)
    core_copy = pltpu.make_async_remote_copy(
        src_ref=sk, dst_ref=rx_core, send_sem=core_send, recv_sem=core_recv,
        device_id=(ind, other), device_id_type=MESH,
    )
    core_copy.start()

    def y_copy(k, c, slot):
        return pltpu.make_async_remote_copy(
            src_ref=ry.at[y, c], dst_ref=ry.at[slot, c],
            send_sem=y_send.at[k, c], recv_sem=y_recv.at[slot, c],
            device_id=(ind, lax.rem(y + k, ny) * CORES + core), device_id_type=MESH,
        )

    def second_chunk(c):
        mine = sketch_chunk(CHUNKS + c) + rx_core[c]
        ry[y, c] = fold(mine).astype(jnp.bfloat16)
        for k in range(1, ny):
            y_copy(k, c, y).start()

    def second(c, carry):
        second_chunk(c)
        return carry

    core_copy.wait_recv()
    lax.fori_loop(0, CHUNKS, second, 0)
    core_copy.wait_send()

    pieces = []
    gram = jnp.zeros((rank, rank), jnp.float32)
    for c in range(CHUNKS):
        for k in range(1, ny):
            y_copy(k, c, lax.rem(y + k, ny)).wait_recv()
        total = ry[0, c].astype(jnp.float32)
        for k in range(1, ny):
            total += ry[k, c].astype(jnp.float32)
        rounded = total.astype(jnp.bfloat16)
        s_out[c] = rounded
        piece = unfold(rounded.astype(jnp.float32))
        pieces.append(piece)
    s_copy = pltpu.make_async_remote_copy(
        src_ref=s_out, dst_ref=s_in, send_sem=s_send, recv_sem=s_recv,
        device_id=(ind, other), device_id_type=MESH,
    )
    s_copy.start()
    mine = jnp.concatenate(pieces, axis=1)
    row_sum = jnp.sum(mine, axis=1, keepdims=True)
    mine = mine.astype(jnp.bfloat16)
    s_cat[1] = mine
    gram = dot_nt(mine, mine)
    pad = jnp.zeros((8, 32 - rank), jnp.float32)
    parts = []
    for g in range(rank // 8):
        parts += [gram[8 * g : 8 * g + 8, :], pad]
    parts.append(jnp.zeros((8, 128 - 4 * rank), jnp.float32))
    rg[gme] = jnp.concatenate(parts, axis=1)

    def g_copy(k, slot):
        to = lax.rem(gme + k, group)
        return pltpu.make_async_remote_copy(
            src_ref=rg.at[gme], dst_ref=rg.at[slot],
            send_sem=g_send.at[k], recv_sem=g_recv.at[slot],
            device_id=(lax.div(to, CORES), y * CORES + lax.rem(to, CORES)),
            device_id_type=MESH,
        )

    def g_start(k, carry):
        g_copy(k, gme).start()
        return carry

    lax.fori_loop(1, group, g_start, 0)

    span = CHUNKS * ci

    def own_half(b, carry):
        qacc[b] = jnp.dot(
            s_cat[1], codes[b, span : 2 * span, :], preferred_element_type=jnp.float32
        )
        return carry

    lax.fori_loop(0, n, own_half, 0)
    s_copy.wait_recv()
    theirs = jnp.concatenate(
        [unfold(s_in[c].astype(jnp.float32)) for c in range(CHUNKS)], axis=1
    )
    row_sum = row_sum + jnp.sum(theirs, axis=1, keepdims=True)
    s_cat[0] = theirs.astype(jnp.bfloat16)

    def rs_copy(k, slot):
        to = lax.rem(ind + k, n)
        return pltpu.make_async_remote_copy(
            src_ref=rs_out.at[to], dst_ref=rs_in.at[slot],
            send_sem=rs_send.at[k], recv_sem=rs_recv.at[slot],
            device_id=(to, snp), device_id_type=MESH,
        )

    def block(b):
        q = qacc[b] + jnp.dot(
            s_cat[0], codes[b, 0:span, :], preferred_element_type=jnp.float32
        )
        return fold(scales[b] * (q - means[b] * row_sum)).astype(jnp.bfloat16)

    def other_half(k, carry):
        b = lax.rem(ind + k, n)
        rs_out[b] = block(b)
        rs_copy(k, ind).start()
        return carry

    lax.fori_loop(1, n, other_half, 0)
    rs_in[ind] = block(ind)

    def g_wait(k, carry):
        g_copy(k, lax.rem(gme + k, group)).wait_recv()
        return carry

    lax.fori_loop(1, group, g_wait, 0)
    packed = lax.fori_loop(1, group, lambda k, t: t + rg[k], rg[0])
    lower_inv = inverse_factor(packed, rank)

    def rs_wait(k, carry):
        rs_copy(k, lax.rem(ind + k, n)).wait_recv()
        return carry

    lax.fori_loop(1, n, rs_wait, 0)
    q = lax.fori_loop(
        1, n, lambda k, t: t + rs_in[k].astype(jnp.float32), rs_in[0].astype(jnp.float32)
    )
    loadings = jnp.dot(
        lower_inv, unfold(q), precision=lax.Precision.HIGHEST,
        preferred_element_type=jnp.float32,
    )
    ag[ind] = fold(loadings).astype(jnp.bfloat16)

    def ag_copy(k, slot):
        return pltpu.make_async_remote_copy(
            src_ref=ag.at[ind], dst_ref=ag.at[slot],
            send_sem=ag_send.at[k], recv_sem=ag_recv.at[slot],
            device_id=(lax.rem(ind + k, n), snp), device_id_type=MESH,
        )

    def ag_start(k, carry):
        ag_copy(k, ind).start()
        return carry

    lax.fori_loop(1, n, ag_start, 0)

    def drain(k, carry):
        ag_copy(k, lax.rem(ind + k, n)).wait_recv()
        rs_copy(k, ind).wait_send()
        return carry

    lax.fori_loop(1, n, drain, 0)
    for b in range(n):
        out_ref[:, b * w : (b + 1) * w] = unfold(ag[b].astype(jnp.float32))

    def drain_ag(k, carry):
        ag_copy(k, ind).wait_send()
        return carry

    lax.fori_loop(1, n, drain_ag, 0)

    def drain_g(k, carry):
        g_copy(k, gme).wait_send()
        return carry

    lax.fori_loop(1, group, drain_g, 0)
    s_copy.wait_send()
    for c in range(CHUNKS):
        for k in range(1, ny):
            y_copy(k, c, y).wait_send()


def on_device(n, ny, genotype, probe, allele_mean, allele_scale):
    word_rows, cols = genotype.shape
    rank = probe.shape[0]
    w = cols // n
    ci = word_rows // (2 * CHUNKS) * PLANES
    group = n * CORES
    f32, b16 = jnp.float32, jnp.bfloat16
    dma = pltpu.SemaphoreType.DMA
    vmem = pl.BlockSpec(memory_space=pltpu.VMEM)
    return pl.pallas_call(
        functools.partial(kernel, n, ny),
        out_shape=jax.ShapeDtypeStruct((rank, cols), f32),
        in_specs=[pl.BlockSpec(memory_space=pl.ANY), vmem, vmem, vmem],
        out_specs=vmem,
        scratch_shapes=[
            pltpu.VMEM((word_rows, cols), jnp.int32),
            pltpu.VMEM((n, PLANES * word_rows, w), b16),
            pltpu.VMEM((n, 2 * rank, w), b16),
            pltpu.VMEM((n, 1, w), f32),
            pltpu.VMEM((n, 1, w), f32),
            pltpu.VMEM((CHUNKS, rank, ci), f32),
            pltpu.VMEM((CHUNKS, rank, ci), f32),
            pltpu.VMEM((ny, CHUNKS, 2 * rank, ci // 2), b16),
            pltpu.VMEM((CHUNKS, 2 * rank, ci // 2), b16),
            pltpu.VMEM((CHUNKS, 2 * rank, ci // 2), b16),
            pltpu.VMEM((2, rank, CHUNKS * ci), b16),
            pltpu.VMEM((group, 8, 128), f32),
            pltpu.VMEM((n, rank, w), f32),
            pltpu.VMEM((n, 2 * rank, w // 2), b16),
            pltpu.VMEM((n, 2 * rank, w // 2), b16),
            pltpu.VMEM((n, 2 * rank, w // 2), b16),
            dma((2 * CHUNKS,)),
            dma, dma,
            dma((ny, CHUNKS)), dma((ny, CHUNKS)),
            dma, dma,
            dma((group,)), dma((group,)),
            dma((n,)), dma((n,)),
            dma((n,)), dma((n,)),
        ],
        compiler_params=pltpu.CompilerParams(
            collective_id=0, has_side_effects=True, vmem_limit_bytes=48 * 1024 * 1024
        ),
        cost_estimate=pl.CostEstimate(
            flops=4 * rank * PLANES * word_rows * cols,
            bytes_accessed=4 * word_rows * cols,
            transcendentals=0,
        ),
    )(genotype, probe, allele_mean.reshape(1, cols), allele_scale.reshape(1, cols))


def solution(mesh):
    n = mesh.shape["ind"]
    ny = mesh.shape["snp"] // CORES
    return jax.shard_map(
        functools.partial(on_device, n, ny),
        mesh=mesh,
        in_specs=(P("ind", "snp"), P(None, "snp"), P("snp"), P("snp")),
        out_specs=P(None, "snp"),
        check_vma=False,
    )
```

```python
import functools

import jax
import jax.numpy as jnp
from jax import lax
from jax.experimental import pallas as pl
from jax.experimental.pallas import tpu as pltpu
from jax.sharding import PartitionSpec as P

MESH = pl.DeviceIdType.MESH
CORES = 2
CHUNKS = 4
PLANES = 4


def fold(x):
    half = x.shape[1] // 2
    return jnp.concatenate([x[:, :half], x[:, half:]], axis=0)


def unfold(x):
    rows = x.shape[0] // 2
    return jnp.concatenate([x[:rows], x[rows:]], axis=1)


def dot_nt(a, b):
    return lax.dot_general(
        a, b, (((1,), (1,)), ((), ())), preferred_element_type=jnp.float32
    )


def inverse_factor(packed, rank):
    groups = rank // 8
    a = jnp.concatenate([packed[:, 32 * g : 32 * g + 32] for g in range(groups)], axis=0)
    shape = (rank, 128)
    row_id = lax.broadcasted_iota(jnp.int32, shape, 0)
    lane_id = lax.broadcasted_iota(jnp.int32, shape, 1)
    eye = jnp.where(lane_id == row_id + 32, 1.0, 0.0).astype(jnp.float32)
    m = jnp.concatenate([a, jnp.zeros((rank, 96), jnp.float32)], axis=1) + eye
    rows1 = lax.broadcasted_iota(jnp.int32, (rank, 1), 0)
    for p in range(rank - 1):
        factor = jnp.where(rows1 > p, m[:, p : p + 1] / m[p : p + 1, p : p + 1], 0.0)
        m = m - factor * m[p : p + 1, :]
    pivots = jnp.sum(jnp.where(lane_id == row_id, m, 0.0), axis=1, keepdims=True)
    return m[:, 32 : 32 + rank] * (1.0 / jnp.sqrt(pivots))


def kernel(
    n, ny, g_hbm, probe_hbm, mean_hbm, scale_hbm, out_ref,
    words, probe_ref, mean_ref, scale_ref, codes, weights, means, scales, sk, rx_core, ry, s_out, s_in, s_cat, row_sums,
    rg, qacc, rs_out, rs_in, ag,
    load_sem, small_sem, core_send, core_recv, y_send, y_recv, s_send, s_recv,
    g_send, g_recv, rs_send, rs_recv, ag_send, ag_recv,
):
    rank, cols = probe_hbm.shape
    w = cols // n
    half = words.shape[0] // 2
    cw = half // CHUNKS
    ci = cw * PLANES
    group = n * CORES
    ind = lax.axis_index("ind")
    snp = lax.axis_index("snp")
    core = lax.rem(snp, CORES)
    y = lax.div(snp, CORES)
    other = snp + 1 - 2 * core
    gme = ind * CORES + core

    def load(c):
        h, k = divmod(c, CHUNKS) if isinstance(c, int) else (lax.div(c, CHUNKS), lax.rem(c, CHUNKS))
        where = jnp.where(h == 0, 1 - core, core)
        row = pl.multiple_of(where * half + k * cw, 8)
        at = pl.multiple_of(c * cw, 8)
        return pltpu.make_async_copy(
            g_hbm.at[pl.ds(row, cw), :], words.at[pl.ds(at, cw), :], load_sem.at[c]
        )

    small = [
        pltpu.make_async_copy(probe_hbm, probe_ref, small_sem.at[0]),
        pltpu.make_async_copy(mean_hbm, mean_ref, small_sem.at[1]),
        pltpu.make_async_copy(scale_hbm, scale_ref, small_sem.at[2]),
    ]
    for copy in small:
        copy.start()
    for c in range(2 * CHUNKS):
        load(c).start()

    barrier = pltpu.get_barrier_semaphore()

    def greet(k, carry):
        to = lax.rem(gme + k, group)
        pl.semaphore_signal(
            barrier, inc=1, device_id=(lax.div(to, CORES), y * CORES + lax.rem(to, CORES)),
            device_id_type=MESH,
        )
        return carry

    lax.fori_loop(1, group, greet, 0)
    for k in range(1, ny):
        pl.semaphore_signal(
            barrier, inc=1, device_id=(ind, lax.rem(y + k, ny) * CORES + core),
            device_id_type=MESH,
        )

    qacc[...] = jnp.zeros_like(qacc)
    for copy in small:
        copy.wait()
    scale = scale_ref[...]
    mean = mean_ref[...]
    scaled = probe_ref[...].astype(jnp.float32) * scale
    const = jnp.sum(scaled * mean, axis=1, keepdims=True)
    high = scaled.astype(jnp.bfloat16).astype(jnp.float32)
    both = jnp.concatenate([high, scaled - high], axis=0).astype(jnp.bfloat16)
    for b in range(n):
        weights[b] = both[:, b * w : (b + 1) * w]
        means[b] = mean[:, b * w : (b + 1) * w]
        scales[b] = scale[:, b * w : (b + 1) * w]

    def sketch_chunk(c):
        load(c).wait()
        at = pl.multiple_of(c * cw, 8)
        total = jnp.zeros((2 * rank, ci), jnp.float32)
        for b in range(n):
            packed = words[pl.ds(at, cw), b * w : (b + 1) * w]
            tile = jnp.concatenate(
                [((packed >> (2 * k)) & 3).astype(jnp.float32) for k in range(PLANES)], axis=0
            ).astype(jnp.bfloat16)
            codes[b, pl.ds(pl.multiple_of(c * ci, 16), ci), :] = tile
            total += dot_nt(weights[b], tile)
        return total[:rank] + total[rank:] - const

    core_copy = pltpu.make_async_remote_copy(
        src_ref=sk.at[0:CHUNKS], dst_ref=rx_core, send_sem=core_send, recv_sem=core_recv,
        device_id=(ind, other), device_id_type=MESH,
    )
    def y_copy(k, c, slot):
        return pltpu.make_async_remote_copy(
            src_ref=ry.at[y, c], dst_ref=ry.at[slot, c],
            send_sem=y_send.at[k, c], recv_sem=y_recv.at[slot, c],
            device_id=(ind, lax.rem(y + k, ny) * CORES + core), device_id_type=MESH,
        )

    def chunk(c, carry):
        sk[c] = sketch_chunk(c)

        @pl.when(c == CHUNKS - 1)
        def _():
            pl.semaphore_wait(barrier, group - 1 + ny - 1)
            core_copy.start()

        @pl.when(c == CHUNKS)
        def _():
            core_copy.wait_recv()

        @pl.when(c >= CHUNKS)
        def _():
            j = c - CHUNKS
            ry[y, j] = fold(sk[c] + rx_core[j]).astype(jnp.bfloat16)
            for k in range(1, ny):
                y_copy(k, j, y).start()

        return carry

    lax.fori_loop(0, 2 * CHUNKS, chunk, 0)
    core_copy.wait_send()

    pieces = []
    gram = jnp.zeros((rank, rank), jnp.float32)
    for c in range(CHUNKS):
        for k in range(1, ny):
            y_copy(k, c, lax.rem(y + k, ny)).wait_recv()
        total = ry[0, c].astype(jnp.float32)
        for k in range(1, ny):
            total += ry[k, c].astype(jnp.float32)
        rounded = total.astype(jnp.bfloat16)
        s_out[c] = rounded
        piece = unfold(rounded.astype(jnp.float32))
        pieces.append(piece)
    s_copy = pltpu.make_async_remote_copy(
        src_ref=s_out, dst_ref=s_in, send_sem=s_send, recv_sem=s_recv,
        device_id=(ind, other), device_id_type=MESH,
    )
    s_copy.start()
    mine = jnp.concatenate(pieces, axis=1)
    row_sums[...] = jnp.broadcast_to(jnp.sum(mine, axis=1, keepdims=True), (rank, 128))
    mine = mine.astype(jnp.bfloat16)
    s_cat[1] = mine
    gram = dot_nt(mine, mine)
    pad = jnp.zeros((8, 32 - rank), jnp.float32)
    parts = []
    for g in range(rank // 8):
        parts += [gram[8 * g : 8 * g + 8, :], pad]
    parts.append(jnp.zeros((8, 128 - 4 * rank), jnp.float32))
    rg[gme] = jnp.concatenate(parts, axis=1)

    def g_copy(k, slot):
        to = lax.rem(gme + k, group)
        return pltpu.make_async_remote_copy(
            src_ref=rg.at[gme], dst_ref=rg.at[slot],
            send_sem=g_send.at[k], recv_sem=g_recv.at[slot],
            device_id=(lax.div(to, CORES), y * CORES + lax.rem(to, CORES)),
            device_id_type=MESH,
        )

    def g_start(k, carry):
        g_copy(k, gme).start()
        return carry

    lax.fori_loop(1, group, g_start, 0)

    span = CHUNKS * ci

    def rs_copy(k, slot):
        to = lax.rem(ind + k, n)
        return pltpu.make_async_remote_copy(
            src_ref=rs_out.at[to], dst_ref=rs_in.at[slot],
            send_sem=rs_send.at[k], recv_sem=rs_recv.at[slot],
            device_id=(to, snp), device_id_type=MESH,
        )

    def product(t, carry):
        later = t > n
        h = jnp.where(later, 0, 1)
        k = jnp.where(later, t - n, t)
        b = lax.rem(ind + k, n)

        @pl.when(t == n + 1)
        def _():
            s_copy.wait_recv()
            theirs = jnp.concatenate(
                [unfold(s_in[c].astype(jnp.float32)) for c in range(CHUNKS)], axis=1
            )
            row_sums[...] += jnp.broadcast_to(
                jnp.sum(theirs, axis=1, keepdims=True), (rank, 128)
            )
            s_cat[0] = theirs.astype(jnp.bfloat16)

        at = pl.multiple_of(h * span, 16)
        q = qacc[b] + jnp.dot(
            s_cat[h], codes[b, pl.ds(at, span), :], preferred_element_type=jnp.float32
        )
        qacc[b] = q

        @pl.when(later)
        def _():
            centred = scales[b] * (qacc[b] - means[b] * row_sums[:, 0:1])
            rs_out[b] = fold(centred).astype(jnp.bfloat16)

        @pl.when(jnp.logical_and(later, k < n))
        def _():
            rs_copy(k, ind).start()

        return carry

    lax.fori_loop(1, 2 * n + 1, product, 0)
    rs_in[ind] = rs_out[ind]

    def g_wait(k, carry):
        g_copy(k, lax.rem(gme + k, group)).wait_recv()
        return carry

    lax.fori_loop(1, group, g_wait, 0)
    packed = lax.fori_loop(1, group, lambda k, t: t + rg[k], rg[0])
    lower_inv = inverse_factor(packed, rank)

    def rs_wait(k, carry):
        rs_copy(k, lax.rem(ind + k, n)).wait_recv()
        return carry

    lax.fori_loop(1, n, rs_wait, 0)
    q = lax.fori_loop(
        1, n, lambda k, t: t + rs_in[k].astype(jnp.float32), rs_in[0].astype(jnp.float32)
    )
    loadings = jnp.dot(
        lower_inv, unfold(q), precision=lax.Precision.HIGHEST,
        preferred_element_type=jnp.float32,
    )
    ag[ind] = fold(loadings).astype(jnp.bfloat16)

    def ag_copy(k, slot):
        return pltpu.make_async_remote_copy(
            src_ref=ag.at[ind], dst_ref=ag.at[slot],
            send_sem=ag_send.at[k], recv_sem=ag_recv.at[slot],
            device_id=(lax.rem(ind + k, n), snp), device_id_type=MESH,
        )

    def ag_start(k, carry):
        ag_copy(k, ind).start()
        return carry

    lax.fori_loop(1, n, ag_start, 0)

    def drain(k, carry):
        ag_copy(k, lax.rem(ind + k, n)).wait_recv()
        rs_copy(k, ind).wait_send()
        return carry

    lax.fori_loop(1, n, drain, 0)
    for b in range(n):
        out_ref[:, b * w : (b + 1) * w] = unfold(ag[b].astype(jnp.float32))

    def drain_ag(k, carry):
        ag_copy(k, ind).wait_send()
        return carry

    lax.fori_loop(1, n, drain_ag, 0)

    def drain_g(k, carry):
        g_copy(k, gme).wait_send()
        return carry

    lax.fori_loop(1, group, drain_g, 0)
    s_copy.wait_send()
    for c in range(CHUNKS):
        for k in range(1, ny):
            y_copy(k, c, y).wait_send()


def on_device(n, ny, genotype, probe, allele_mean, allele_scale):
    word_rows, cols = genotype.shape
    rank = probe.shape[0]
    w = cols // n
    ci = word_rows // (2 * CHUNKS) * PLANES
    group = n * CORES
    f32, b16 = jnp.float32, jnp.bfloat16
    dma = pltpu.SemaphoreType.DMA
    vmem = pl.BlockSpec(memory_space=pltpu.VMEM)
    return pl.pallas_call(
        functools.partial(kernel, n, ny),
        out_shape=jax.ShapeDtypeStruct((rank, cols), f32),
        in_specs=[pl.BlockSpec(memory_space=pltpu.HBM)] * 4,
        out_specs=vmem,
        scratch_shapes=[
            pltpu.VMEM((word_rows, cols), jnp.int32),
            pltpu.VMEM((rank, cols), b16),
            pltpu.VMEM((1, cols), f32),
            pltpu.VMEM((1, cols), f32),
            pltpu.VMEM((n, PLANES * word_rows, w), b16),
            pltpu.VMEM((n, 2 * rank, w), b16),
            pltpu.VMEM((n, 1, w), f32),
            pltpu.VMEM((n, 1, w), f32),
            pltpu.VMEM((2 * CHUNKS, rank, ci), f32),
            pltpu.VMEM((CHUNKS, rank, ci), f32),
            pltpu.VMEM((ny, CHUNKS, 2 * rank, ci // 2), b16),
            pltpu.VMEM((CHUNKS, 2 * rank, ci // 2), b16),
            pltpu.VMEM((CHUNKS, 2 * rank, ci // 2), b16),
            pltpu.VMEM((2, rank, CHUNKS * ci), b16),
            pltpu.VMEM((rank, 128), f32),
            pltpu.VMEM((group, 8, 128), f32),
            pltpu.VMEM((n, rank, w), f32),
            pltpu.VMEM((n, 2 * rank, w // 2), b16),
            pltpu.VMEM((n, 2 * rank, w // 2), b16),
            pltpu.VMEM((n, 2 * rank, w // 2), b16),
            dma((2 * CHUNKS,)),
            dma((3,)),
            dma, dma,
            dma((ny, CHUNKS)), dma((ny, CHUNKS)),
            dma, dma,
            dma((group,)), dma((group,)),
            dma((n,)), dma((n,)),
            dma((n,)), dma((n,)),
        ],
        compiler_params=pltpu.CompilerParams(
            collective_id=0, has_side_effects=True, vmem_limit_bytes=63 * 1024 * 1024
        ),
        cost_estimate=pl.CostEstimate(
            flops=4 * rank * PLANES * word_rows * cols,
            bytes_accessed=4 * word_rows * cols,
            transcendentals=0,
        ),
    )(genotype, probe, allele_mean.reshape(1, cols), allele_scale.reshape(1, cols))


def solution(mesh):
    n = mesh.shape["ind"]
    ny = mesh.shape["snp"] // CORES
    return jax.shard_map(
        functools.partial(on_device, n, ny),
        mesh=mesh,
        in_specs=(P("ind", "snp"), P(None, "snp"), P("snp"), P("snp")),
        out_specs=P(None, "snp"),
        check_vma=False,
    )
```

```python
import functools

import jax
import jax.numpy as jnp
from jax import lax
from jax.experimental import pallas as pl
from jax.experimental.pallas import tpu as pltpu
from jax.sharding import PartitionSpec as P

MESH = pl.DeviceIdType.MESH
CORES = 2
CHUNKS = 4
PLANES = 4


def fold(x):
    half = x.shape[1] // 2
    return jnp.concatenate([x[:, :half], x[:, half:]], axis=0)


def unfold(x):
    rows = x.shape[0] // 2
    return jnp.concatenate([x[:rows], x[rows:]], axis=1)


def dot_nt(a, b):
    return lax.dot_general(
        a, b, (((1,), (1,)), ((), ())), preferred_element_type=jnp.float32
    )


def inverse_factor(packed, rank):
    groups = rank // 8
    a = jnp.concatenate([packed[:, 32 * g : 32 * g + 32] for g in range(groups)], axis=0)
    shape = (rank, 128)
    row_id = lax.broadcasted_iota(jnp.int32, shape, 0)
    lane_id = lax.broadcasted_iota(jnp.int32, shape, 1)
    eye = jnp.where(lane_id == row_id + 32, 1.0, 0.0).astype(jnp.float32)
    m = jnp.concatenate([a, jnp.zeros((rank, 96), jnp.float32)], axis=1) + eye
    rows1 = lax.broadcasted_iota(jnp.int32, (rank, 1), 0)
    for p in range(rank - 1):
        factor = jnp.where(rows1 > p, m[:, p : p + 1] / m[p : p + 1, p : p + 1], 0.0)
        m = m - factor * m[p : p + 1, :]
    pivots = jnp.sum(jnp.where(lane_id == row_id, m, 0.0), axis=1, keepdims=True)
    return m[:, 32 : 32 + rank] * (1.0 / jnp.sqrt(pivots))


def kernel(
    n, ny, g_hbm, probe_hbm, mean_hbm, scale_hbm, out_ref,
    words, probe_ref, mean_ref, scale_ref, codes, weights, means, scales, sk, rx_core, ry, s_out, s_in, s_cat,
    rg, qacc, rs_out, rs_in, ag,
    load_sem, small_sem, core_send, core_recv, y_send, y_recv, s_send, s_recv,
    g_send, g_recv, rs_send, rs_recv, ag_send, ag_recv,
):
    rank, cols = probe_hbm.shape
    w = cols // n
    half = words.shape[0] // 2
    cw = half // CHUNKS
    ci = cw * PLANES
    group = n * CORES
    ind = lax.axis_index("ind")
    snp = lax.axis_index("snp")
    core = lax.rem(snp, CORES)
    y = lax.div(snp, CORES)
    other = snp + 1 - 2 * core
    gme = ind * CORES + core

    def load(c):
        h, k = divmod(c, CHUNKS) if isinstance(c, int) else (lax.div(c, CHUNKS), lax.rem(c, CHUNKS))
        where = jnp.where(h == 0, 1 - core, core)
        row = pl.multiple_of(where * half + k * cw, 8)
        at = pl.multiple_of(c * cw, 8)
        return pltpu.make_async_copy(
            g_hbm.at[pl.ds(row, cw), :], words.at[pl.ds(at, cw), :], load_sem.at[c]
        )

    small = [
        pltpu.make_async_copy(probe_hbm, probe_ref, small_sem.at[0]),
        pltpu.make_async_copy(mean_hbm, mean_ref, small_sem.at[1]),
        pltpu.make_async_copy(scale_hbm, scale_ref, small_sem.at[2]),
    ]
    for copy in small:
        copy.start()
    for c in range(2 * CHUNKS):
        load(c).start()

    barrier = pltpu.get_barrier_semaphore()

    def greet(k, carry):
        to = lax.rem(gme + k, group)
        pl.semaphore_signal(
            barrier, inc=1, device_id=(lax.div(to, CORES), y * CORES + lax.rem(to, CORES)),
            device_id_type=MESH,
        )
        return carry

    lax.fori_loop(1, group, greet, 0)
    for k in range(1, ny):
        pl.semaphore_signal(
            barrier, inc=1, device_id=(ind, lax.rem(y + k, ny) * CORES + core),
            device_id_type=MESH,
        )

    qacc[...] = jnp.zeros_like(qacc)
    for copy in small:
        copy.wait()
    scale = scale_ref[...]
    mean = mean_ref[...]
    scaled = probe_ref[...].astype(jnp.float32) * scale
    const = jnp.sum(scaled * mean, axis=1, keepdims=True)
    high = scaled.astype(jnp.bfloat16).astype(jnp.float32)
    both = jnp.concatenate([high, scaled - high], axis=0).T.astype(jnp.bfloat16)
    for b in range(n):
        weights[b] = both[b * w : (b + 1) * w, :]
        means[b] = mean[:, b * w : (b + 1) * w]
        scales[b] = scale[:, b * w : (b + 1) * w]

    def sketch_chunk(c):
        load(c).wait()
        at = pl.multiple_of(c * cw, 8)
        total = jnp.zeros((ci, 2 * rank), jnp.float32)
        for b in range(n):
            packed = words[pl.ds(at, cw), b * w : (b + 1) * w]
            tile = jnp.concatenate(
                [((packed >> (2 * k)) & 3).astype(jnp.float32) for k in range(PLANES)], axis=0
            ).astype(jnp.bfloat16)
            codes[b, pl.ds(pl.multiple_of(c * ci, 16), ci), :] = tile
            total += jnp.dot(tile, weights[b], preferred_element_type=jnp.float32)
        total = total.T
        return total[:rank] + total[rank:] - const

    core_copy = pltpu.make_async_remote_copy(
        src_ref=sk.at[0:CHUNKS], dst_ref=rx_core, send_sem=core_send, recv_sem=core_recv,
        device_id=(ind, other), device_id_type=MESH,
    )
    def y_copy(k, c, slot):
        return pltpu.make_async_remote_copy(
            src_ref=ry.at[y, c], dst_ref=ry.at[slot, c],
            send_sem=y_send.at[k, c], recv_sem=y_recv.at[slot, c],
            device_id=(ind, lax.rem(y + k, ny) * CORES + core), device_id_type=MESH,
        )

    def chunk(c, carry):
        sk[c] = sketch_chunk(c)

        @pl.when(c == CHUNKS - 1)
        def _():
            pl.semaphore_wait(barrier, group - 1 + ny - 1)
            core_copy.start()

        @pl.when(c == CHUNKS)
        def _():
            core_copy.wait_recv()

        @pl.when(c >= CHUNKS)
        def _():
            j = c - CHUNKS
            ry[y, j] = fold(sk[c] + rx_core[j]).astype(jnp.bfloat16)
            for k in range(1, ny):
                y_copy(k, j, y).start()

        return carry

    lax.fori_loop(0, 2 * CHUNKS, chunk, 0)
    core_copy.wait_send()

    def s_copy(c):
        return pltpu.make_async_remote_copy(
            src_ref=s_out.at[c], dst_ref=s_in.at[c], send_sem=s_send.at[c], recv_sem=s_recv.at[c],
            device_id=(ind, other), device_id_type=MESH,
        )

    def g_copy(k, slot):
        to = lax.rem(gme + k, group)
        return pltpu.make_async_remote_copy(
            src_ref=rg.at[gme], dst_ref=rg.at[slot],
            send_sem=g_send.at[k], recv_sem=g_recv.at[slot],
            device_id=(lax.div(to, CORES), y * CORES + lax.rem(to, CORES)),
            device_id_type=MESH,
        )

    def g_start(k, carry):
        g_copy(k, gme).start()
        return carry

    span = CHUNKS * ci

    def own_half(c, carry):
        gram, row_sum = carry
        for k in range(1, ny):
            y_copy(k, c, lax.rem(y + k, ny)).wait_recv()
        total = ry[0, c].astype(jnp.float32)
        for k in range(1, ny):
            total += ry[k, c].astype(jnp.float32)
        rounded = total.astype(jnp.bfloat16)
        s_out[c] = rounded
        s_copy(c).start()
        piece = unfold(rounded.astype(jnp.float32))
        row_sum = row_sum + jnp.sum(piece, axis=1, keepdims=True)
        piece = piece.astype(jnp.bfloat16)
        gram = gram + dot_nt(piece, piece)

        @pl.when(c == CHUNKS - 1)
        def _():
            pad = jnp.zeros((8, 32 - rank), jnp.float32)
            parts = []
            for g in range(rank // 8):
                parts += [gram[8 * g : 8 * g + 8, :], pad]
            parts.append(jnp.zeros((8, 128 - 4 * rank), jnp.float32))
            rg[gme] = jnp.concatenate(parts, axis=1)
            lax.fori_loop(1, group, g_start, 0)

        at = pl.multiple_of(span + c * ci, 16)
        for b in range(n):
            qacc[b] += jnp.dot(
                piece, codes[b, pl.ds(at, ci), :], preferred_element_type=jnp.float32
            )
        return gram, row_sum

    ignored, row_sum = lax.fori_loop(
        0, CHUNKS, own_half,
        (jnp.zeros((rank, rank), jnp.float32), jnp.zeros((rank, 1), jnp.float32)),
    )
    theirs = []
    for c in range(CHUNKS):
        s_copy(c).wait_recv()
        theirs.append(unfold(s_in[c].astype(jnp.float32)))
    theirs = jnp.concatenate(theirs, axis=1)
    row_sum = row_sum + jnp.sum(theirs, axis=1, keepdims=True)
    s_cat[...] = theirs.astype(jnp.bfloat16)

    def rs_copy(k, slot):
        to = lax.rem(ind + k, n)
        return pltpu.make_async_remote_copy(
            src_ref=rs_out.at[to], dst_ref=rs_in.at[slot],
            send_sem=rs_send.at[k], recv_sem=rs_recv.at[slot],
            device_id=(to, snp), device_id_type=MESH,
        )

    def product(k, carry):
        b = lax.rem(ind + k, n)
        q = qacc[b] + jnp.dot(
            s_cat[...], codes[b, 0:span, :], preferred_element_type=jnp.float32
        )
        rs_out[b] = fold(scales[b] * (q - means[b] * row_sum)).astype(jnp.bfloat16)

        @pl.when(k < n)
        def _():
            rs_copy(k, ind).start()

        return carry

    lax.fori_loop(1, n + 1, product, 0)
    rs_in[ind] = rs_out[ind]

    def g_wait(k, carry):
        g_copy(k, lax.rem(gme + k, group)).wait_recv()
        return carry

    lax.fori_loop(1, group, g_wait, 0)
    packed = lax.fori_loop(1, group, lambda k, t: t + rg[k], rg[0])
    lower_inv = inverse_factor(packed, rank)

    def rs_wait(k, carry):
        rs_copy(k, lax.rem(ind + k, n)).wait_recv()
        return carry

    lax.fori_loop(1, n, rs_wait, 0)
    q = lax.fori_loop(
        1, n, lambda k, t: t + rs_in[k].astype(jnp.float32), rs_in[0].astype(jnp.float32)
    )
    loadings = jnp.dot(
        lower_inv, unfold(q), precision=lax.Precision.HIGHEST,
        preferred_element_type=jnp.float32,
    )
    ag[ind] = fold(loadings).astype(jnp.bfloat16)

    def ag_copy(k, slot):
        return pltpu.make_async_remote_copy(
            src_ref=ag.at[ind], dst_ref=ag.at[slot],
            send_sem=ag_send.at[k], recv_sem=ag_recv.at[slot],
            device_id=(lax.rem(ind + k, n), snp), device_id_type=MESH,
        )

    def ag_start(k, carry):
        ag_copy(k, ind).start()
        return carry

    lax.fori_loop(1, n, ag_start, 0)

    def drain(k, carry):
        ag_copy(k, lax.rem(ind + k, n)).wait_recv()
        rs_copy(k, ind).wait_send()
        return carry

    lax.fori_loop(1, n, drain, 0)
    for b in range(n):
        out_ref[:, b * w : (b + 1) * w] = unfold(ag[b].astype(jnp.float32)).astype(jnp.bfloat16)

    def drain_ag(k, carry):
        ag_copy(k, ind).wait_send()
        return carry

    lax.fori_loop(1, n, drain_ag, 0)

    def drain_g(k, carry):
        g_copy(k, gme).wait_send()
        return carry

    lax.fori_loop(1, group, drain_g, 0)
    for c in range(CHUNKS):
        s_copy(c).wait_send()
        for k in range(1, ny):
            y_copy(k, c, y).wait_send()


def on_device(n, ny, genotype, probe, allele_mean, allele_scale):
    word_rows, cols = genotype.shape
    rank = probe.shape[0]
    w = cols // n
    ci = word_rows // (2 * CHUNKS) * PLANES
    group = n * CORES
    f32, b16 = jnp.float32, jnp.bfloat16
    dma = pltpu.SemaphoreType.DMA
    vmem = pl.BlockSpec(memory_space=pltpu.VMEM)
    return pl.pallas_call(
        functools.partial(kernel, n, ny),
        out_shape=jax.ShapeDtypeStruct((rank, cols), b16),
        in_specs=[pl.BlockSpec(memory_space=pltpu.HBM)] * 4,
        out_specs=vmem,
        scratch_shapes=[
            pltpu.VMEM((word_rows, cols), jnp.int32),
            pltpu.VMEM((rank, cols), b16),
            pltpu.VMEM((1, cols), f32),
            pltpu.VMEM((1, cols), f32),
            pltpu.VMEM((n, PLANES * word_rows, w), b16),
            pltpu.VMEM((n, w, 2 * rank), b16),
            pltpu.VMEM((n, 1, w), f32),
            pltpu.VMEM((n, 1, w), f32),
            pltpu.VMEM((2 * CHUNKS, rank, ci), f32),
            pltpu.VMEM((CHUNKS, rank, ci), f32),
            pltpu.VMEM((ny, CHUNKS, 2 * rank, ci // 2), b16),
            pltpu.VMEM((CHUNKS, 2 * rank, ci // 2), b16),
            pltpu.VMEM((CHUNKS, 2 * rank, ci // 2), b16),
            pltpu.VMEM((rank, CHUNKS * ci), b16),
            pltpu.VMEM((group, 8, 128), f32),
            pltpu.VMEM((n, rank, w), f32),
            pltpu.VMEM((n, 2 * rank, w // 2), b16),
            pltpu.VMEM((n, 2 * rank, w // 2), b16),
            pltpu.VMEM((n, 2 * rank, w // 2), b16),
            dma((2 * CHUNKS,)),
            dma((3,)),
            dma, dma,
            dma((ny, CHUNKS)), dma((ny, CHUNKS)),
            dma((CHUNKS,)), dma((CHUNKS,)),
            dma((group,)), dma((group,)),
            dma((n,)), dma((n,)),
            dma((n,)), dma((n,)),
        ],
        compiler_params=pltpu.CompilerParams(
            collective_id=0, has_side_effects=True, vmem_limit_bytes=63 * 1024 * 1024
        ),
        cost_estimate=pl.CostEstimate(
            flops=4 * rank * PLANES * word_rows * cols,
            bytes_accessed=4 * word_rows * cols,
            transcendentals=0,
        ),
    )(genotype, probe, allele_mean.reshape(1, cols), allele_scale.reshape(1, cols)).astype(f32)


def solution(mesh):
    n = mesh.shape["ind"]
    ny = mesh.shape["snp"] // CORES
    return jax.shard_map(
        functools.partial(on_device, n, ny),
        mesh=mesh,
        in_specs=(P("ind", "snp"), P(None, "snp"), P("snp"), P("snp")),
        out_specs=P(None, "snp"),
        check_vma=False,
    )
```

```python
import functools

import jax
import jax.numpy as jnp
from jax import lax
from jax.experimental import pallas as pl
from jax.experimental.pallas import tpu as pltpu
from jax.sharding import PartitionSpec as P

MESH = pl.DeviceIdType.MESH
CORES = 2
CHUNKS = 4
PLANES = 4
SUBS = 2


def fold(x):
    half = x.shape[1] // 2
    return jnp.concatenate([x[:, :half], x[:, half:]], axis=0)


def unfold(x):
    rows = x.shape[0] // 2
    return jnp.concatenate([x[:rows], x[rows:]], axis=1)


def dot_nt(a, b):
    return lax.dot_general(
        a, b, (((1,), (1,)), ((), ())), preferred_element_type=jnp.float32
    )


def inverse_factor(packed, rank):
    groups = rank // 8
    a = jnp.concatenate([packed[:, 32 * g : 32 * g + 32] for g in range(groups)], axis=0)
    shape = (rank, 128)
    row_id = lax.broadcasted_iota(jnp.int32, shape, 0)
    lane_id = lax.broadcasted_iota(jnp.int32, shape, 1)
    eye = jnp.where(lane_id == row_id + 32, 1.0, 0.0).astype(jnp.float32)
    m = jnp.concatenate([a, jnp.zeros((rank, 96), jnp.float32)], axis=1) + eye
    for start in range(0, rank, 8):
        spread = [jnp.broadcast_to(m[:, p : p + 1], shape) for p in range(start, start + 8)]
        for j in range(8):
            p = start + j
            column = spread[j]
            factor = jnp.where(row_id > p, column * (1.0 / column[p : p + 1, :]), 0.0)
            m = m - factor * m[p : p + 1, :]
            for l in range(j + 1, 8):
                spread[l] = spread[l] - factor * spread[l][p : p + 1, :]
    pivots = jnp.sum(jnp.where(lane_id == row_id, m, 0.0), axis=1, keepdims=True)
    return m[:, 32 : 32 + rank] * (1.0 / jnp.sqrt(pivots))


def kernel(
    n, ny, g_hbm, probe_hbm, mean_hbm, scale_hbm, out_ref,
    words, probe_ref, mean_ref, scale_ref, codes, weights, means, scales, sk, rx_core, ry, s_out, s_in, s_cat,
    rg, qacc, rs_out, rs_in, ag,
    load_sem, small_sem, core_send, core_recv, y_send, y_recv, s_send, s_recv,
    g_send, g_recv, rs_send, rs_recv, ag_send, ag_recv,
):
    rank, cols = probe_hbm.shape
    w = cols // n
    half = words.shape[0] // 2
    cw = half // CHUNKS
    ci = cw * PLANES
    sw = cw // SUBS
    si = ci // SUBS
    ind = lax.axis_index("ind")
    snp = lax.axis_index("snp")
    core = lax.rem(snp, CORES)
    y = lax.div(snp, CORES)
    other = snp + 1 - 2 * core

    def load(c):
        h, k = divmod(c, CHUNKS) if isinstance(c, int) else (lax.div(c, CHUNKS), lax.rem(c, CHUNKS))
        where = jnp.where(h == 0, 1 - core, core)
        row = pl.multiple_of(where * half + k * cw, 8)
        at = pl.multiple_of(c * cw, 8)
        return pltpu.make_async_copy(
            g_hbm.at[pl.ds(row, cw), :], words.at[pl.ds(at, cw), :], load_sem.at[c]
        )

    small = [
        pltpu.make_async_copy(probe_hbm, probe_ref, small_sem.at[0]),
        pltpu.make_async_copy(mean_hbm, mean_ref, small_sem.at[1]),
        pltpu.make_async_copy(scale_hbm, scale_ref, small_sem.at[2]),
    ]
    for copy in small:
        copy.start()
    for c in range(2 * CHUNKS):
        load(c).start()

    barrier = pltpu.get_barrier_semaphore()

    def greet(k, carry):
        pl.semaphore_signal(
            barrier, inc=1, device_id=(lax.rem(ind + k, n), snp), device_id_type=MESH
        )
        return carry

    lax.fori_loop(1, n, greet, 0)
    pl.semaphore_signal(barrier, inc=1, device_id=(ind, other), device_id_type=MESH)
    for k in range(1, ny):
        pl.semaphore_signal(
            barrier, inc=1, device_id=(ind, lax.rem(y + k, ny) * CORES + core),
            device_id_type=MESH,
        )

    qacc[...] = jnp.zeros_like(qacc)
    for copy in small:
        copy.wait()
    scale = scale_ref[...]
    mean = mean_ref[...]
    scaled = probe_ref[...].astype(jnp.float32) * scale
    const = jnp.sum(scaled * mean, axis=1, keepdims=True)
    high = scaled.astype(jnp.bfloat16).astype(jnp.float32)
    both = jnp.concatenate([high, scaled - high], axis=0).T.astype(jnp.bfloat16)
    for b in range(n):
        weights[b] = both[b * w : (b + 1) * w, :]
        means[b] = mean[:, b * w : (b + 1) * w]
        scales[b] = scale[:, b * w : (b + 1) * w]

    lane = lax.broadcasted_iota(jnp.int32, (1, ci), 1)
    plane = lax.rem(lane, si) // sw
    plane_scale = jnp.where(
        plane < 2, jnp.where(plane == 0, 1.0, 1 / 4), jnp.where(plane == 2, 1 / 16, 1 / 64)
    ).astype(jnp.float32)

    def sketch_chunk(c):
        load(c).wait()
        at = pl.multiple_of(c * cw, 8)
        pieces = []
        for sub in range(SUBS):
            total = jnp.zeros((si, 2 * rank), jnp.float32)
            for b in range(n):
                packed = words[pl.ds(at + sub * sw, sw), b * w : (b + 1) * w]
                tile = jnp.concatenate(
                    [
                        (packed & (3 << (2 * k))).astype(jnp.float32).astype(jnp.bfloat16)
                        for k in range(PLANES)
                    ],
                    axis=0,
                )
                codes[b, pl.ds(pl.multiple_of(c * ci + sub * si, 16), si), :] = tile
                total += jnp.dot(tile, weights[b], preferred_element_type=jnp.float32)
            pieces.append(total.T)
        total = jnp.concatenate(pieces, axis=1)
        return (total[:rank] + total[rank:]) * plane_scale - const

    core_copy = pltpu.make_async_remote_copy(
        src_ref=sk.at[0:CHUNKS], dst_ref=rx_core, send_sem=core_send, recv_sem=core_recv,
        device_id=(ind, other), device_id_type=MESH,
    )
    def y_copy(k, c, slot):
        return pltpu.make_async_remote_copy(
            src_ref=ry.at[y, c], dst_ref=ry.at[slot, c],
            send_sem=y_send.at[k, c], recv_sem=y_recv.at[slot, c],
            device_id=(ind, lax.rem(y + k, ny) * CORES + core), device_id_type=MESH,
        )

    def chunk(c, carry):
        sk[c] = sketch_chunk(c)

        @pl.when(c == CHUNKS - 1)
        def _():
            pl.semaphore_wait(barrier, n - 1 + 1 + ny - 1)
            core_copy.start()

        @pl.when(c == CHUNKS)
        def _():
            core_copy.wait_recv()

        @pl.when(c >= CHUNKS)
        def _():
            j = c - CHUNKS
            ry[y, j] = fold(sk[c] + rx_core[j]).astype(jnp.bfloat16)
            for k in range(1, ny):
                y_copy(k, j, y).start()

        return carry

    lax.fori_loop(0, 2 * CHUNKS, chunk, 0)

    def s_copy(c):
        return pltpu.make_async_remote_copy(
            src_ref=s_out.at[c], dst_ref=s_in.at[c], send_sem=s_send.at[c], recv_sem=s_recv.at[c],
            device_id=(ind, other), device_id_type=MESH,
        )

    def g_copy(k, slot):
        return pltpu.make_async_remote_copy(
            src_ref=rg.at[ind], dst_ref=rg.at[slot],
            send_sem=g_send.at[k], recv_sem=g_recv.at[slot],
            device_id=(lax.rem(ind + k, n), snp), device_id_type=MESH,
        )

    def g_start(k, carry):
        g_copy(k, ind).start()
        return carry

    span = CHUNKS * ci

    def own_half(c, carry):
        gram, row_sum = carry
        for k in range(1, ny):
            y_copy(k, c, lax.rem(y + k, ny)).wait_recv()
        total = ry[0, c].astype(jnp.float32)
        for k in range(1, ny):
            total += ry[k, c].astype(jnp.float32)
        rounded = total.astype(jnp.bfloat16)
        s_out[c] = rounded
        s_copy(c).start()
        piece = unfold(rounded.astype(jnp.float32))
        row_sum = row_sum + jnp.sum(piece, axis=1, keepdims=True)
        exact = piece.astype(jnp.bfloat16)
        gram = gram + dot_nt(exact, exact)
        piece = (piece * plane_scale).astype(jnp.bfloat16)
        at = pl.multiple_of(span + c * ci, 16)
        for b in range(n):
            qacc[b] += jnp.dot(
                piece, codes[b, pl.ds(at, ci), :], preferred_element_type=jnp.float32
            )
        return gram, row_sum

    gram, row_sum = lax.fori_loop(
        0, CHUNKS, own_half,
        (jnp.zeros((rank, rank), jnp.float32), jnp.zeros((rank, 1), jnp.float32)),
    )
    theirs = []
    for c in range(CHUNKS):
        s_copy(c).wait_recv()
        theirs.append(unfold(s_in[c].astype(jnp.float32)))
    theirs = jnp.concatenate(theirs, axis=1)
    row_sum = row_sum + jnp.sum(theirs, axis=1, keepdims=True)
    exact = theirs.astype(jnp.bfloat16)
    gram = gram + dot_nt(exact, exact)
    pad = jnp.zeros((8, 32 - rank), jnp.float32)
    parts = []
    for g in range(rank // 8):
        parts += [gram[8 * g : 8 * g + 8, :], pad]
    parts.append(jnp.zeros((8, 128 - 4 * rank), jnp.float32))
    rg[ind] = jnp.concatenate(parts, axis=1)
    lax.fori_loop(1, n, g_start, 0)
    s_cat[...] = (theirs * jnp.concatenate([plane_scale] * CHUNKS, axis=1)).astype(jnp.bfloat16)

    def rs_copy(k, slot):
        to = lax.rem(ind + k, n)
        return pltpu.make_async_remote_copy(
            src_ref=rs_out.at[to], dst_ref=rs_in.at[slot],
            send_sem=rs_send.at[k], recv_sem=rs_recv.at[slot],
            device_id=(to, snp), device_id_type=MESH,
        )

    def product(k, carry):
        b = lax.rem(ind + k, n)
        q = qacc[b] + jnp.dot(
            s_cat[...], codes[b, 0:span, :], preferred_element_type=jnp.float32
        )
        rs_out[b] = fold(scales[b] * (q - means[b] * row_sum)).astype(jnp.bfloat16)

        @pl.when(k < n)
        def _():
            rs_copy(k, ind).start()

        return carry

    lax.fori_loop(1, n + 1, product, 0)
    rs_in[ind] = rs_out[ind]

    def g_wait(k, carry):
        g_copy(k, lax.rem(ind + k, n)).wait_recv()
        return carry

    lax.fori_loop(1, n, g_wait, 0)
    packed = lax.fori_loop(1, n, lambda k, t: t + rg[k], rg[0])
    lower_inv = inverse_factor(packed, rank)

    def rs_wait(k, carry):
        rs_copy(k, lax.rem(ind + k, n)).wait_recv()
        return carry

    lax.fori_loop(1, n, rs_wait, 0)
    q = lax.fori_loop(
        1, n, lambda k, t: t + rs_in[k].astype(jnp.float32), rs_in[0].astype(jnp.float32)
    )
    loadings = jnp.dot(
        lower_inv, unfold(q), precision=lax.Precision.HIGHEST,
        preferred_element_type=jnp.float32,
    )
    ag[ind] = fold(loadings).astype(jnp.bfloat16)

    def ag_copy(k, slot):
        return pltpu.make_async_remote_copy(
            src_ref=ag.at[ind], dst_ref=ag.at[slot],
            send_sem=ag_send.at[k], recv_sem=ag_recv.at[slot],
            device_id=(lax.rem(ind + k, n), snp), device_id_type=MESH,
        )

    def ag_start(k, carry):
        ag_copy(k, ind).start()
        return carry

    lax.fori_loop(1, n, ag_start, 0)

    def drain(k, carry):
        rs_copy(k, ind).wait_send()
        g_copy(k, ind).wait_send()
        return carry

    lax.fori_loop(1, n, drain, 0)
    core_copy.wait_send()
    for c in range(CHUNKS):
        s_copy(c).wait_send()
        for k in range(1, ny):
            y_copy(k, c, y).wait_send()

    def arrive(k, carry):
        ag_copy(k, lax.rem(ind + k, n)).wait_recv()
        return carry

    lax.fori_loop(1, n, arrive, 0)
    for b in range(n):
        out_ref[:, b * w : (b + 1) * w] = unfold(ag[b].astype(jnp.float32)).astype(jnp.bfloat16)

    def drain_ag(k, carry):
        ag_copy(k, ind).wait_send()
        return carry

    lax.fori_loop(1, n, drain_ag, 0)


def on_device(n, ny, genotype, probe, allele_mean, allele_scale):
    word_rows, cols = genotype.shape
    rank = probe.shape[0]
    w = cols // n
    ci = word_rows // (2 * CHUNKS) * PLANES
    f32, b16 = jnp.float32, jnp.bfloat16
    dma = pltpu.SemaphoreType.DMA
    vmem = pl.BlockSpec(memory_space=pltpu.VMEM)
    return pl.pallas_call(
        functools.partial(kernel, n, ny),
        out_shape=jax.ShapeDtypeStruct((rank, cols), b16),
        in_specs=[pl.BlockSpec(memory_space=pltpu.HBM)] * 4,
        out_specs=vmem,
        scratch_shapes=[
            pltpu.VMEM((word_rows, cols), jnp.int32),
            pltpu.VMEM((rank, cols), b16),
            pltpu.VMEM((1, cols), f32),
            pltpu.VMEM((1, cols), f32),
            pltpu.VMEM((n, PLANES * word_rows, w), b16),
            pltpu.VMEM((n, w, 2 * rank), b16),
            pltpu.VMEM((n, 1, w), f32),
            pltpu.VMEM((n, 1, w), f32),
            pltpu.VMEM((2 * CHUNKS, rank, ci), f32),
            pltpu.VMEM((CHUNKS, rank, ci), f32),
            pltpu.VMEM((ny, CHUNKS, 2 * rank, ci // 2), b16),
            pltpu.VMEM((CHUNKS, 2 * rank, ci // 2), b16),
            pltpu.VMEM((CHUNKS, 2 * rank, ci // 2), b16),
            pltpu.VMEM((rank, CHUNKS * ci), b16),
            pltpu.VMEM((n, 8, 128), f32),
            pltpu.VMEM((n, rank, w), f32),
            pltpu.VMEM((n, 2 * rank, w // 2), b16),
            pltpu.VMEM((n, 2 * rank, w // 2), b16),
            pltpu.VMEM((n, 2 * rank, w // 2), b16),
            dma((2 * CHUNKS,)),
            dma((3,)),
            dma, dma,
            dma((ny, CHUNKS)), dma((ny, CHUNKS)),
            dma((CHUNKS,)), dma((CHUNKS,)),
            dma((n,)), dma((n,)),
            dma((n,)), dma((n,)),
            dma((n,)), dma((n,)),
        ],
        compiler_params=pltpu.CompilerParams(
            collective_id=0, has_side_effects=True, vmem_limit_bytes=63 * 1024 * 1024
        ),
        cost_estimate=pl.CostEstimate(
            flops=4 * rank * PLANES * word_rows * cols,
            bytes_accessed=4 * word_rows * cols,
            transcendentals=0,
        ),
    )(genotype, probe, allele_mean.reshape(1, cols), allele_scale.reshape(1, cols)).astype(f32)


def solution(mesh):
    n = mesh.shape["ind"]
    ny = mesh.shape["snp"] // CORES
    return jax.shard_map(
        functools.partial(on_device, n, ny),
        mesh=mesh,
        in_specs=(P("ind", "snp"), P(None, "snp"), P("snp"), P("snp")),
        out_specs=P(None, "snp"),
        check_vma=False,
    )
```

```python
import functools

import jax
import jax.numpy as jnp
from jax import lax
from jax.experimental import pallas as pl
from jax.experimental.pallas import tpu as pltpu
from jax.sharding import PartitionSpec as P

MESH = pl.DeviceIdType.MESH
CORES = 2
CHUNKS = 4
PLANES = 4
SUBS = 1


def fold(x):
    half = x.shape[1] // 2
    return jnp.concatenate([x[:, :half], x[:, half:]], axis=0)


def unfold(x):
    rows = x.shape[0] // 2
    return jnp.concatenate([x[:rows], x[rows:]], axis=1)


def dot_nt(a, b):
    return lax.dot_general(
        a, b, (((1,), (1,)), ((), ())), preferred_element_type=jnp.float32
    )


def inverse_factor(packed, rank):
    groups = rank // 8
    a = jnp.concatenate([packed[:, 32 * g : 32 * g + 32] for g in range(groups)], axis=0)
    shape = (rank, 128)
    row_id = lax.broadcasted_iota(jnp.int32, shape, 0)
    lane_id = lax.broadcasted_iota(jnp.int32, shape, 1)
    eye = jnp.where(lane_id == row_id + 32, 1.0, 0.0).astype(jnp.float32)
    m = jnp.concatenate([a, jnp.zeros((rank, 96), jnp.float32)], axis=1) + eye
    for start in range(0, rank, 8):
        spread = [jnp.broadcast_to(m[:, p : p + 1], shape) for p in range(start, start + 8)]
        for j in range(8):
            p = start + j
            column = spread[j]
            factor = jnp.where(row_id > p, column * (1.0 / column[p : p + 1, :]), 0.0)
            m = m - factor * m[p : p + 1, :]
            for l in range(j + 1, 8):
                spread[l] = spread[l] - factor * spread[l][p : p + 1, :]
    pivots = jnp.sum(jnp.where(lane_id == row_id, m, 0.0), axis=1, keepdims=True)
    return m[:, 32 : 32 + rank] * (1.0 / jnp.sqrt(pivots))


def kernel(
    n, ny, g_hbm, probe_hbm, mean_hbm, scale_hbm, out_ref,
    words, probe_ref, mean_ref, scale_ref, codes, weights, means, scales, sk, rx_core, ry, s_out, s_in, s_cat,
    rg, qacc, rs_out, rs_in, ag,
    load_sem, small_sem, core_send, core_recv, y_send, y_recv, s_send, s_recv,
    g_send, g_recv, rs_send, rs_recv, ag_send, ag_recv,
):
    rank, cols = probe_hbm.shape
    w = cols // n
    half = words.shape[0] // 2
    cw = half // CHUNKS
    ci = cw * PLANES
    sw = cw // SUBS
    si = ci // SUBS
    ind = lax.axis_index("ind")
    snp = lax.axis_index("snp")
    core = lax.rem(snp, CORES)
    y = lax.div(snp, CORES)
    other = snp + 1 - 2 * core

    def load(c):
        h, k = divmod(c, CHUNKS) if isinstance(c, int) else (lax.div(c, CHUNKS), lax.rem(c, CHUNKS))
        where = jnp.where(h == 0, 1 - core, core)
        row = pl.multiple_of(where * half + k * cw, 8)
        at = pl.multiple_of(c * cw, 8)
        return pltpu.make_async_copy(
            g_hbm.at[pl.ds(row, cw), :], words.at[pl.ds(at, cw), :], load_sem.at[c]
        )

    small = [
        pltpu.make_async_copy(probe_hbm, probe_ref, small_sem.at[0]),
        pltpu.make_async_copy(mean_hbm, mean_ref, small_sem.at[1]),
        pltpu.make_async_copy(scale_hbm, scale_ref, small_sem.at[2]),
    ]
    for copy in small:
        copy.start()
    for c in range(2 * CHUNKS):
        load(c).start()

    barrier = pltpu.get_barrier_semaphore()

    def greet(k, carry):
        pl.semaphore_signal(
            barrier, inc=1, device_id=(lax.rem(ind + k, n), snp), device_id_type=MESH
        )
        return carry

    lax.fori_loop(1, n, greet, 0)
    pl.semaphore_signal(barrier, inc=1, device_id=(ind, other), device_id_type=MESH)
    for k in range(1, ny):
        pl.semaphore_signal(
            barrier, inc=1, device_id=(ind, lax.rem(y + k, ny) * CORES + core),
            device_id_type=MESH,
        )

    qacc[...] = jnp.zeros_like(qacc)
    for copy in small:
        copy.wait()
    scale = scale_ref[...]
    mean = mean_ref[...]
    scaled = probe_ref[...].astype(jnp.float32) * scale
    const = jnp.sum(scaled * mean, axis=1, keepdims=True)
    high = scaled.astype(jnp.bfloat16).astype(jnp.float32)
    both = jnp.concatenate([high, scaled - high], axis=0).astype(jnp.bfloat16)
    for b in range(n):
        weights[b] = both[:, b * w : (b + 1) * w]
        means[b] = mean[:, b * w : (b + 1) * w]
        scales[b] = scale[:, b * w : (b + 1) * w]

    lane = lax.broadcasted_iota(jnp.int32, (1, ci), 1)
    plane = lax.rem(lane, si) // sw
    plane_scale = jnp.where(
        plane < 2, jnp.where(plane == 0, 1.0, 1 / 4), jnp.where(plane == 2, 1 / 16, 1 / 64)
    ).astype(jnp.float32)

    def sketch_chunk(c):
        load(c).wait()
        at = pl.multiple_of(c * cw, 8)
        pieces = []
        for sub in range(SUBS):
            total = jnp.zeros((2 * rank, si), jnp.float32)
            for b in range(n):
                packed = words[pl.ds(at + sub * sw, sw), b * w : (b + 1) * w]
                tile = jnp.concatenate(
                    [
                        (packed & (3 << (2 * k))).astype(jnp.float32).astype(jnp.bfloat16)
                        for k in range(PLANES)
                    ],
                    axis=0,
                )
                codes[b, pl.ds(pl.multiple_of(c * ci + sub * si, 16), si), :] = tile
                total += dot_nt(weights[b], tile)
            pieces.append(total)
        total = jnp.concatenate(pieces, axis=1)
        return (total[:rank] + total[rank:]) * plane_scale - const

    core_copy = pltpu.make_async_remote_copy(
        src_ref=sk.at[0:CHUNKS], dst_ref=rx_core, send_sem=core_send, recv_sem=core_recv,
        device_id=(ind, other), device_id_type=MESH,
    )
    def y_copy(k, c, slot):
        return pltpu.make_async_remote_copy(
            src_ref=ry.at[y, c], dst_ref=ry.at[slot, c],
            send_sem=y_send.at[k, c], recv_sem=y_recv.at[slot, c],
            device_id=(ind, lax.rem(y + k, ny) * CORES + core), device_id_type=MESH,
        )

    def chunk(c, carry):
        sk[c] = sketch_chunk(c)

        @pl.when(c == CHUNKS - 1)
        def _():
            pl.semaphore_wait(barrier, n - 1 + 1 + ny - 1)
            core_copy.start()

        @pl.when(c == CHUNKS)
        def _():
            core_copy.wait_recv()

        @pl.when(c >= CHUNKS)
        def _():
            j = c - CHUNKS
            ry[y, j] = fold(sk[c] + rx_core[j]).astype(jnp.bfloat16)
            for k in range(1, ny):
                y_copy(k, j, y).start()

        return carry

    lax.fori_loop(0, 2 * CHUNKS, chunk, 0)

    def s_copy(c):
        return pltpu.make_async_remote_copy(
            src_ref=s_out.at[c], dst_ref=s_in.at[c], send_sem=s_send.at[c], recv_sem=s_recv.at[c],
            device_id=(ind, other), device_id_type=MESH,
        )

    def g_copy(k, slot):
        return pltpu.make_async_remote_copy(
            src_ref=rg.at[ind], dst_ref=rg.at[slot],
            send_sem=g_send.at[k], recv_sem=g_recv.at[slot],
            device_id=(lax.rem(ind + k, n), snp), device_id_type=MESH,
        )

    def g_start(k, carry):
        g_copy(k, ind).start()
        return carry

    span = CHUNKS * ci

    def own_half(c, carry):
        gram, row_sum = carry
        for k in range(1, ny):
            y_copy(k, c, lax.rem(y + k, ny)).wait_recv()
        total = ry[0, c].astype(jnp.float32)
        for k in range(1, ny):
            total += ry[k, c].astype(jnp.float32)
        rounded = total.astype(jnp.bfloat16)
        s_out[c] = rounded
        s_copy(c).start()
        piece = unfold(rounded.astype(jnp.float32))
        row_sum = row_sum + jnp.sum(piece, axis=1, keepdims=True)
        exact = piece.astype(jnp.bfloat16)
        gram = gram + dot_nt(exact, exact)
        piece = (piece * plane_scale).astype(jnp.bfloat16)
        at = pl.multiple_of(span + c * ci, 16)
        for b in range(n):
            qacc[b] += jnp.dot(
                piece, codes[b, pl.ds(at, ci), :], preferred_element_type=jnp.float32
            )
        return gram, row_sum

    gram, row_sum = lax.fori_loop(
        0, CHUNKS, own_half,
        (jnp.zeros((rank, rank), jnp.float32), jnp.zeros((rank, 1), jnp.float32)),
    )
    theirs = []
    for c in range(CHUNKS):
        s_copy(c).wait_recv()
        theirs.append(unfold(s_in[c].astype(jnp.float32)))
    theirs = jnp.concatenate(theirs, axis=1)
    row_sum = row_sum + jnp.sum(theirs, axis=1, keepdims=True)
    exact = theirs.astype(jnp.bfloat16)
    gram = gram + dot_nt(exact, exact)
    pad = jnp.zeros((8, 32 - rank), jnp.float32)
    parts = []
    for g in range(rank // 8):
        parts += [gram[8 * g : 8 * g + 8, :], pad]
    parts.append(jnp.zeros((8, 128 - 4 * rank), jnp.float32))
    rg[ind] = jnp.concatenate(parts, axis=1)
    lax.fori_loop(1, n, g_start, 0)
    s_cat[...] = (theirs * jnp.concatenate([plane_scale] * CHUNKS, axis=1)).astype(jnp.bfloat16)

    def rs_copy(k, slot):
        to = lax.rem(ind + k, n)
        return pltpu.make_async_remote_copy(
            src_ref=rs_out.at[to], dst_ref=rs_in.at[slot],
            send_sem=rs_send.at[k], recv_sem=rs_recv.at[slot],
            device_id=(to, snp), device_id_type=MESH,
        )

    def product(k, carry):
        b = lax.rem(ind + k, n)
        q = qacc[b] + jnp.dot(
            s_cat[...], codes[b, 0:span, :], preferred_element_type=jnp.float32
        )
        rs_out[b] = fold(scales[b] * (q - means[b] * row_sum)).astype(jnp.bfloat16)

        @pl.when(k < n)
        def _():
            rs_copy(k, ind).start()

        return carry

    lax.fori_loop(1, n + 1, product, 0)
    rs_in[ind] = rs_out[ind]

    def g_wait(k, carry):
        g_copy(k, lax.rem(ind + k, n)).wait_recv()
        return carry

    lax.fori_loop(1, n, g_wait, 0)
    packed = lax.fori_loop(1, n, lambda k, t: t + rg[k], rg[0])
    lower_inv = inverse_factor(packed, rank)

    def rs_wait(k, carry):
        rs_copy(k, lax.rem(ind + k, n)).wait_recv()
        return carry

    lax.fori_loop(1, n, rs_wait, 0)
    q = lax.fori_loop(
        1, n, lambda k, t: t + rs_in[k].astype(jnp.float32), rs_in[0].astype(jnp.float32)
    )
    loadings = jnp.dot(
        lower_inv, unfold(q), precision=lax.Precision.HIGHEST,
        preferred_element_type=jnp.float32,
    )
    ag[ind] = fold(loadings).astype(jnp.bfloat16)

    def ag_copy(k, slot):
        return pltpu.make_async_remote_copy(
            src_ref=ag.at[ind], dst_ref=ag.at[slot],
            send_sem=ag_send.at[k], recv_sem=ag_recv.at[slot],
            device_id=(lax.rem(ind + k, n), snp), device_id_type=MESH,
        )

    def ag_start(k, carry):
        ag_copy(k, ind).start()
        return carry

    lax.fori_loop(1, n, ag_start, 0)

    def drain(k, carry):
        rs_copy(k, ind).wait_send()
        g_copy(k, ind).wait_send()
        return carry

    lax.fori_loop(1, n, drain, 0)
    core_copy.wait_send()
    for c in range(CHUNKS):
        s_copy(c).wait_send()
        for k in range(1, ny):
            y_copy(k, c, y).wait_send()

    def arrive(k, carry):
        ag_copy(k, lax.rem(ind + k, n)).wait_recv()
        return carry

    lax.fori_loop(1, n, arrive, 0)
    for b in range(n):
        out_ref[:, b * w : (b + 1) * w] = unfold(ag[b].astype(jnp.float32)).astype(jnp.bfloat16)

    def drain_ag(k, carry):
        ag_copy(k, ind).wait_send()
        return carry

    lax.fori_loop(1, n, drain_ag, 0)


def on_device(n, ny, genotype, probe, allele_mean, allele_scale):
    word_rows, cols = genotype.shape
    rank = probe.shape[0]
    w = cols // n
    ci = word_rows // (2 * CHUNKS) * PLANES
    f32, b16 = jnp.float32, jnp.bfloat16
    dma = pltpu.SemaphoreType.DMA
    vmem = pl.BlockSpec(memory_space=pltpu.VMEM)
    operands = genotype, probe, allele_mean.reshape(1, cols), allele_scale.reshape(1, cols)
    return pl.pallas_call(
        functools.partial(kernel, n, ny),
        out_shape=jax.ShapeDtypeStruct((rank, cols), b16),
        in_specs=[pl.BlockSpec(memory_space=pltpu.HBM)] * 4,
        out_specs=vmem,
        scratch_shapes=[
            pltpu.VMEM((word_rows, cols), jnp.int32),
            pltpu.VMEM((rank, cols), b16),
            pltpu.VMEM((1, cols), f32),
            pltpu.VMEM((1, cols), f32),
            pltpu.VMEM((n, PLANES * word_rows, w), b16),
            pltpu.VMEM((n, 2 * rank, w), b16),
            pltpu.VMEM((n, 1, w), f32),
            pltpu.VMEM((n, 1, w), f32),
            pltpu.VMEM((2 * CHUNKS, rank, ci), f32),
            pltpu.VMEM((CHUNKS, rank, ci), f32),
            pltpu.VMEM((ny, CHUNKS, 2 * rank, ci // 2), b16),
            pltpu.VMEM((CHUNKS, 2 * rank, ci // 2), b16),
            pltpu.VMEM((CHUNKS, 2 * rank, ci // 2), b16),
            pltpu.VMEM((rank, CHUNKS * ci), b16),
            pltpu.VMEM((n, 8, 128), f32),
            pltpu.VMEM((n, rank, w), f32),
            pltpu.VMEM((n, 2 * rank, w // 2), b16),
            pltpu.VMEM((n, 2 * rank, w // 2), b16),
            pltpu.VMEM((n, 2 * rank, w // 2), b16),
            dma((2 * CHUNKS,)),
            dma((3,)),
            dma, dma,
            dma((ny, CHUNKS)), dma((ny, CHUNKS)),
            dma((CHUNKS,)), dma((CHUNKS,)),
            dma((n,)), dma((n,)),
            dma((n,)), dma((n,)),
            dma((n,)), dma((n,)),
        ],
        compiler_params=pltpu.CompilerParams(
            collective_id=0, has_side_effects=True, vmem_limit_bytes=48 * 1024 * 1024
        ),
        cost_estimate=pl.CostEstimate(
            flops=4 * rank * PLANES * word_rows * cols,
            bytes_accessed=4 * word_rows * cols,
            transcendentals=0,
        ),
    )(*[pltpu.with_memory_space_constraint(x, pltpu.HBM) for x in operands]).astype(f32)


def solution(mesh):
    n = mesh.shape["ind"]
    ny = mesh.shape["snp"] // CORES
    return jax.shard_map(
        functools.partial(on_device, n, ny),
        mesh=mesh,
        in_specs=(P("ind", "snp"), P(None, "snp"), P("snp"), P("snp")),
        out_specs=P(None, "snp"),
        check_vma=False,
    )
```

```python
import functools

import jax
import jax.numpy as jnp
from jax import lax
from jax.experimental import pallas as pl
from jax.experimental.pallas import tpu as pltpu
from jax.sharding import PartitionSpec as P

MESH = pl.DeviceIdType.MESH
CORES = 2
CHUNKS = 4
PLANES = 4
SUBS = 1


def fold(x):
    half = x.shape[1] // 2
    return jnp.concatenate([x[:, :half], x[:, half:]], axis=0)


def unfold(x):
    rows = x.shape[0] // 2
    return jnp.concatenate([x[:rows], x[rows:]], axis=1)


def dot_nt(a, b):
    return lax.dot_general(
        a, b, (((1,), (1,)), ((), ())), preferred_element_type=jnp.float32
    )


def inverse_factor(packed, rank):
    groups = rank // 8
    a = jnp.concatenate([packed[:, 32 * g : 32 * g + 32] for g in range(groups)], axis=0)
    shape = (rank, 128)
    row_id = lax.broadcasted_iota(jnp.int32, shape, 0)
    lane_id = lax.broadcasted_iota(jnp.int32, shape, 1)
    eye = jnp.where(lane_id == row_id + 32, 1.0, 0.0).astype(jnp.float32)
    m = jnp.concatenate([a, jnp.zeros((rank, 96), jnp.float32)], axis=1) + eye
    for start in range(0, rank, 8):
        spread = [jnp.broadcast_to(m[:, p : p + 1], shape) for p in range(start, start + 8)]
        for j in range(8):
            p = start + j
            column = spread[j]
            factor = jnp.where(row_id > p, column * (1.0 / column[p : p + 1, :]), 0.0)
            m = m - factor * m[p : p + 1, :]
            for l in range(j + 1, 8):
                spread[l] = spread[l] - factor * spread[l][p : p + 1, :]
    pivots = jnp.sum(jnp.where(lane_id == row_id, m, 0.0), axis=1, keepdims=True)
    return m[:, 32 : 32 + rank] * (1.0 / jnp.sqrt(pivots))


def kernel(
    n, ny, g_hbm, probe_hbm, mean_hbm, scale_hbm, out_ref,
    words, probe_ref, mean_ref, scale_ref, codes, weights, means, scales, sk, rx_core, ry, s_out, s_in, s_cat,
    rg, qacc, rs_out, rs_in, ag,
    load_sem, small_sem, core_send, core_recv, y_send, y_recv, s_send, s_recv,
    g_send, g_recv, rs_send, rs_recv, ag_send, ag_recv,
):
    rank, cols = probe_hbm.shape
    w = cols // n
    half = words.shape[0] // 2
    cw = half // CHUNKS
    ci = cw * PLANES
    sw = cw // SUBS
    si = ci // SUBS
    ind = lax.axis_index("ind")
    snp = lax.axis_index("snp")
    core = lax.rem(snp, CORES)
    y = lax.div(snp, CORES)
    other = snp + 1 - 2 * core

    def load(c):
        h, k = divmod(c, CHUNKS) if isinstance(c, int) else (lax.div(c, CHUNKS), lax.rem(c, CHUNKS))
        where = jnp.where(h == 0, 1 - core, core)
        row = pl.multiple_of(where * half + k * cw, 8)
        at = pl.multiple_of(c * cw, 8)
        return pltpu.make_async_copy(
            g_hbm.at[pl.ds(row, cw), :], words.at[pl.ds(at, cw), :], load_sem.at[c]
        )

    small = [
        pltpu.make_async_copy(probe_hbm, probe_ref, small_sem.at[0]),
        pltpu.make_async_copy(mean_hbm, mean_ref, small_sem.at[1]),
        pltpu.make_async_copy(scale_hbm, scale_ref, small_sem.at[2]),
    ]
    for copy in small:
        copy.start()
    for c in range(2 * CHUNKS):
        load(c).start()

    barrier = pltpu.get_barrier_semaphore()

    def greet(k, carry):
        pl.semaphore_signal(
            barrier, inc=1, device_id=(lax.rem(ind + k, n), snp), device_id_type=MESH
        )
        return carry

    lax.fori_loop(1, n, greet, 0)
    pl.semaphore_signal(barrier, inc=1, device_id=(ind, other), device_id_type=MESH)
    for k in range(1, ny):
        pl.semaphore_signal(
            barrier, inc=1, device_id=(ind, lax.rem(y + k, ny) * CORES + core),
            device_id_type=MESH,
        )

    qacc[...] = jnp.zeros_like(qacc)
    for copy in small:
        copy.wait()
    scale = scale_ref[...]
    mean = mean_ref[...]
    scaled = probe_ref[...].astype(jnp.float32) * scale
    const = jnp.sum(scaled * mean, axis=1, keepdims=True)
    high = scaled.astype(jnp.bfloat16).astype(jnp.float32)
    both = jnp.concatenate([high, scaled - high], axis=0).astype(jnp.bfloat16)
    for b in range(n):
        weights[b] = both[:, b * w : (b + 1) * w]
        means[b] = mean[:, b * w : (b + 1) * w]
        scales[b] = scale[:, b * w : (b + 1) * w]

    lane = lax.broadcasted_iota(jnp.int32, (1, ci), 1)
    plane = lax.rem(lane, si) // sw
    plane_scale = jnp.where(
        plane < 2, jnp.where(plane == 0, 1.0, 1 / 4), jnp.where(plane == 2, 1 / 16, 1 / 64)
    ).astype(jnp.float32)

    def sketch_chunk(c):
        load(c).wait()
        at = pl.multiple_of(c * cw, 8)
        pieces = []
        for sub in range(SUBS):
            total = jnp.zeros((2 * rank, si), jnp.float32)
            for b in range(n):
                packed = words[pl.ds(at + sub * sw, sw), b * w : (b + 1) * w]
                tile = jnp.concatenate(
                    [
                        (packed & (3 << (2 * k))).astype(jnp.float32).astype(jnp.bfloat16)
                        for k in range(PLANES)
                    ],
                    axis=0,
                )
                codes[b, pl.ds(pl.multiple_of(c * ci + sub * si, 16), si), :] = tile
                total += dot_nt(weights[b], tile)
            pieces.append(total)
        total = jnp.concatenate(pieces, axis=1)
        return (total[:rank] + total[rank:]) * plane_scale - const

    def core_copy(c):
        return pltpu.make_async_remote_copy(
            src_ref=sk.at[c], dst_ref=rx_core.at[c], send_sem=core_send.at[c],
            recv_sem=core_recv.at[c], device_id=(ind, other), device_id_type=MESH,
        )

    def y_copy(k, c, slot):
        return pltpu.make_async_remote_copy(
            src_ref=ry.at[y, c], dst_ref=ry.at[slot, c],
            send_sem=y_send.at[k, c], recv_sem=y_recv.at[slot, c],
            device_id=(ind, lax.rem(y + k, ny) * CORES + core), device_id_type=MESH,
        )

    def chunk(c, carry):
        sk[c] = sketch_chunk(c)

        @pl.when(c == 0)
        def _():
            pl.semaphore_wait(barrier, n - 1 + 1 + ny - 1)

        @pl.when(c < CHUNKS)
        def _():
            core_copy(c).start()

        @pl.when(c >= CHUNKS)
        def _():
            j = c - CHUNKS
            core_copy(j).wait_recv()
            ry[y, j] = fold(sk[c] + rx_core[j]).astype(jnp.bfloat16)
            for k in range(1, ny):
                y_copy(k, j, y).start()

        return carry

    lax.fori_loop(0, 2 * CHUNKS, chunk, 0)

    def s_copy(c):
        return pltpu.make_async_remote_copy(
            src_ref=s_out.at[c], dst_ref=s_in.at[c], send_sem=s_send.at[c], recv_sem=s_recv.at[c],
            device_id=(ind, other), device_id_type=MESH,
        )

    def g_copy(k, slot):
        return pltpu.make_async_remote_copy(
            src_ref=rg.at[ind], dst_ref=rg.at[slot],
            send_sem=g_send.at[k], recv_sem=g_recv.at[slot],
            device_id=(lax.rem(ind + k, n), snp), device_id_type=MESH,
        )

    def g_start(k, carry):
        g_copy(k, ind).start()
        return carry

    span = CHUNKS * ci

    def own_half(c, carry):
        gram, row_sum = carry
        for k in range(1, ny):
            y_copy(k, c, lax.rem(y + k, ny)).wait_recv()
        total = ry[0, c].astype(jnp.float32)
        for k in range(1, ny):
            total += ry[k, c].astype(jnp.float32)
        rounded = total.astype(jnp.bfloat16)
        s_out[c] = rounded
        s_copy(c).start()
        piece = unfold(rounded.astype(jnp.float32))
        row_sum = row_sum + jnp.sum(piece, axis=1, keepdims=True)
        exact = piece.astype(jnp.bfloat16)
        gram = gram + dot_nt(exact, exact)
        piece = (piece * plane_scale).astype(jnp.bfloat16)
        at = pl.multiple_of(span + c * ci, 16)
        for b in range(n):
            qacc[b] += jnp.dot(
                piece, codes[b, pl.ds(at, ci), :], preferred_element_type=jnp.float32
            )
        return gram, row_sum

    gram, row_sum = lax.fori_loop(
        0, CHUNKS, own_half,
        (jnp.zeros((rank, rank), jnp.float32), jnp.zeros((rank, 1), jnp.float32)),
    )

    def their_piece(c, gram, row_sum):
        s_copy(c).wait_recv()
        piece = unfold(s_in[c].astype(jnp.float32))
        exact = piece.astype(jnp.bfloat16)
        row_sum = row_sum + jnp.sum(piece, axis=1, keepdims=True)
        return (piece * plane_scale).astype(jnp.bfloat16), gram + dot_nt(exact, exact), row_sum

    def their_half(c, carry):
        piece, gram, row_sum = their_piece(c, *carry)
        at = pl.multiple_of(c * ci, 16)
        for b in range(n):
            qacc[b] += jnp.dot(
                piece, codes[b, pl.ds(at, ci), :], preferred_element_type=jnp.float32
            )
        return gram, row_sum

    gram, row_sum = lax.fori_loop(0, CHUNKS - 1, their_half, (gram, row_sum))
    last, gram, row_sum = their_piece(CHUNKS - 1, gram, row_sum)
    s_cat[...] = last
    pad = jnp.zeros((8, 32 - rank), jnp.float32)
    parts = []
    for g in range(rank // 8):
        parts += [gram[8 * g : 8 * g + 8, :], pad]
    parts.append(jnp.zeros((8, 128 - 4 * rank), jnp.float32))
    rg[ind] = jnp.concatenate(parts, axis=1)
    lax.fori_loop(1, n, g_start, 0)

    def rs_copy(k, slot):
        to = lax.rem(ind + k, n)
        return pltpu.make_async_remote_copy(
            src_ref=rs_out.at[to], dst_ref=rs_in.at[slot],
            send_sem=rs_send.at[k], recv_sem=rs_recv.at[slot],
            device_id=(to, snp), device_id_type=MESH,
        )

    def product(k, carry):
        b = lax.rem(ind + k, n)
        q = qacc[b] + jnp.dot(
            s_cat[...], codes[b, span - ci : span, :], preferred_element_type=jnp.float32
        )
        rs_out[b] = fold(scales[b] * (q - means[b] * row_sum)).astype(jnp.bfloat16)

        @pl.when(k < n)
        def _():
            rs_copy(k, ind).start()

        return carry

    lax.fori_loop(1, n + 1, product, 0)
    rs_in[ind] = rs_out[ind]

    def g_wait(k, carry):
        g_copy(k, lax.rem(ind + k, n)).wait_recv()
        return carry

    lax.fori_loop(1, n, g_wait, 0)
    packed = lax.fori_loop(1, n, lambda k, t: t + rg[k], rg[0])
    lower_inv = inverse_factor(packed, rank)

    def rs_wait(k, carry):
        rs_copy(k, lax.rem(ind + k, n)).wait_recv()
        return carry

    lax.fori_loop(1, n, rs_wait, 0)
    q = lax.fori_loop(
        1, n, lambda k, t: t + rs_in[k].astype(jnp.float32), rs_in[0].astype(jnp.float32)
    )
    loadings = jnp.dot(
        lower_inv, unfold(q), precision=lax.Precision.HIGHEST,
        preferred_element_type=jnp.float32,
    )
    ag[ind] = fold(loadings).astype(jnp.bfloat16)

    def ag_copy(k, slot):
        return pltpu.make_async_remote_copy(
            src_ref=ag.at[ind], dst_ref=ag.at[slot],
            send_sem=ag_send.at[k], recv_sem=ag_recv.at[slot],
            device_id=(lax.rem(ind + k, n), snp), device_id_type=MESH,
        )

    def ag_start(k, carry):
        ag_copy(k, ind).start()
        return carry

    lax.fori_loop(1, n, ag_start, 0)

    def drain(k, carry):
        rs_copy(k, ind).wait_send()
        g_copy(k, ind).wait_send()
        return carry

    lax.fori_loop(1, n, drain, 0)
    for c in range(CHUNKS):
        core_copy(c).wait_send()
        s_copy(c).wait_send()
        for k in range(1, ny):
            y_copy(k, c, y).wait_send()

    for b in range(n):
        @pl.when(ind != b)
        def _():
            ag_copy(1, b).wait_recv()

        out_ref[:, b * w : (b + 1) * w] = unfold(ag[b].astype(jnp.float32)).astype(jnp.bfloat16)

    def drain_ag(k, carry):
        ag_copy(k, ind).wait_send()
        return carry

    lax.fori_loop(1, n, drain_ag, 0)


def on_device(n, ny, genotype, probe, allele_mean, allele_scale):
    word_rows, cols = genotype.shape
    rank = probe.shape[0]
    w = cols // n
    ci = word_rows // (2 * CHUNKS) * PLANES
    f32, b16 = jnp.float32, jnp.bfloat16
    dma = pltpu.SemaphoreType.DMA
    vmem = pl.BlockSpec(memory_space=pltpu.VMEM)
    operands = genotype, probe, allele_mean.reshape(1, cols), allele_scale.reshape(1, cols)
    return pl.pallas_call(
        functools.partial(kernel, n, ny),
        out_shape=jax.ShapeDtypeStruct((rank, cols), b16),
        in_specs=[pl.BlockSpec(memory_space=pltpu.HBM)] * 4,
        out_specs=vmem,
        scratch_shapes=[
            pltpu.VMEM((word_rows, cols), jnp.int32),
            pltpu.VMEM((rank, cols), b16),
            pltpu.VMEM((1, cols), f32),
            pltpu.VMEM((1, cols), f32),
            pltpu.VMEM((n, PLANES * word_rows, w), b16),
            pltpu.VMEM((n, 2 * rank, w), b16),
            pltpu.VMEM((n, 1, w), f32),
            pltpu.VMEM((n, 1, w), f32),
            pltpu.VMEM((2 * CHUNKS, rank, ci), f32),
            pltpu.VMEM((CHUNKS, rank, ci), f32),
            pltpu.VMEM((ny, CHUNKS, 2 * rank, ci // 2), b16),
            pltpu.VMEM((CHUNKS, 2 * rank, ci // 2), b16),
            pltpu.VMEM((CHUNKS, 2 * rank, ci // 2), b16),
            pltpu.VMEM((rank, ci), b16),
            pltpu.VMEM((n, 8, 128), f32),
            pltpu.VMEM((n, rank, w), f32),
            pltpu.VMEM((n, 2 * rank, w // 2), b16),
            pltpu.VMEM((n, 2 * rank, w // 2), b16),
            pltpu.VMEM((n, 2 * rank, w // 2), b16),
            dma((2 * CHUNKS,)),
            dma((3,)),
            dma((CHUNKS,)), dma((CHUNKS,)),
            dma((ny, CHUNKS)), dma((ny, CHUNKS)),
            dma((CHUNKS,)), dma((CHUNKS,)),
            dma((n,)), dma((n,)),
            dma((n,)), dma((n,)),
            dma((n,)), dma((n,)),
        ],
        compiler_params=pltpu.CompilerParams(
            collective_id=0, has_side_effects=True, vmem_limit_bytes=48 * 1024 * 1024
        ),
        cost_estimate=pl.CostEstimate(
            flops=4 * rank * PLANES * word_rows * cols,
            bytes_accessed=4 * word_rows * cols,
            transcendentals=0,
        ),
    )(*[pltpu.with_memory_space_constraint(x, pltpu.HBM) for x in operands]).astype(f32)


def solution(mesh):
    n = mesh.shape["ind"]
    ny = mesh.shape["snp"] // CORES
    return jax.shard_map(
        functools.partial(on_device, n, ny),
        mesh=mesh,
        in_specs=(P("ind", "snp"), P(None, "snp"), P("snp"), P("snp")),
        out_specs=P(None, "snp"),
        check_vma=False,
    )
```

```python
import functools

import jax
import jax.numpy as jnp
from jax import lax
from jax.experimental import pallas as pl
from jax.experimental.pallas import tpu as pltpu
from jax.sharding import PartitionSpec as P

MESH = pl.DeviceIdType.MESH
CORES = 2
CHUNKS = 4
PLANES = 4
SUBS = 1


def fold(x):
    half = x.shape[1] // 2
    return jnp.concatenate([x[:, :half], x[:, half:]], axis=0)


def unfold(x):
    rows = x.shape[0] // 2
    return jnp.concatenate([x[:rows], x[rows:]], axis=1)


def dot_nt(a, b):
    return lax.dot_general(
        a, b, (((1,), (1,)), ((), ())), preferred_element_type=jnp.float32
    )


def inverse_factor(packed, rank):
    groups = rank // 8
    a = jnp.concatenate([packed[:, 32 * g : 32 * g + 32] for g in range(groups)], axis=0)
    shape = (rank, 128)
    row_id = lax.broadcasted_iota(jnp.int32, shape, 0)
    lane_id = lax.broadcasted_iota(jnp.int32, shape, 1)
    eye = jnp.where(lane_id == row_id + 32, 1.0, 0.0).astype(jnp.float32)
    m = jnp.concatenate([a, jnp.zeros((rank, 96), jnp.float32)], axis=1) + eye
    for start in range(0, rank, 8):
        spread = [jnp.broadcast_to(m[:, p : p + 1], shape) for p in range(start, start + 8)]
        for j in range(8):
            p = start + j
            column = spread[j]
            factor = jnp.where(row_id > p, column * (1.0 / column[p : p + 1, :]), 0.0)
            m = m - factor * m[p : p + 1, :]
            for l in range(j + 1, 8):
                spread[l] = spread[l] - factor * spread[l][p : p + 1, :]
    pivots = jnp.sum(jnp.where(lane_id == row_id, m, 0.0), axis=1, keepdims=True)
    return m[:, 32 : 32 + rank] * (1.0 / jnp.sqrt(pivots))


def kernel(
    n, ny, g_hbm, probe_hbm, mean_hbm, scale_hbm, out_ref,
    words, probe_ref, mean_ref, scale_ref, codes, weights, means, scales, sk, rx_core, ry, s_out, s_in, s_cat,
    rg, qacc, rs_out, rs_in, ag,
    load_sem, small_sem, core_send, core_recv, y_send, y_recv, s_send, s_recv,
    g_send, g_recv, rs_send, rs_recv, ag_send, ag_recv,
):
    rank, cols = probe_hbm.shape
    w = cols // n
    half = words.shape[0] // 2
    cw = half // CHUNKS
    ci = cw * PLANES
    sw = cw // SUBS
    si = ci // SUBS
    ind = lax.axis_index("ind")
    snp = lax.axis_index("snp")
    core = lax.rem(snp, CORES)
    y = lax.div(snp, CORES)
    other = snp + 1 - 2 * core

    def load(c):
        h, k = divmod(c, CHUNKS) if isinstance(c, int) else (lax.div(c, CHUNKS), lax.rem(c, CHUNKS))
        where = jnp.where(h == 0, 1 - core, core)
        row = pl.multiple_of(where * half + k * cw, 8)
        at = pl.multiple_of(c * cw, 8)
        return pltpu.make_async_copy(
            g_hbm.at[pl.ds(row, cw), :], words.at[pl.ds(at, cw), :], load_sem.at[c]
        )

    small = [
        pltpu.make_async_copy(probe_hbm, probe_ref, small_sem.at[0]),
        pltpu.make_async_copy(mean_hbm, mean_ref, small_sem.at[1]),
        pltpu.make_async_copy(scale_hbm, scale_ref, small_sem.at[2]),
    ]
    for copy in small:
        copy.start()
    for c in range(2 * CHUNKS):
        load(c).start()

    barrier = pltpu.get_barrier_semaphore()

    def greet(k, carry):
        pl.semaphore_signal(
            barrier, inc=1, device_id=(lax.rem(ind + k, n), snp), device_id_type=MESH
        )
        return carry

    lax.fori_loop(1, n, greet, 0)
    pl.semaphore_signal(barrier, inc=1, device_id=(ind, other), device_id_type=MESH)
    for k in range(1, ny):
        pl.semaphore_signal(
            barrier, inc=1, device_id=(ind, lax.rem(y + k, ny) * CORES + core),
            device_id_type=MESH,
        )

    qacc[...] = jnp.zeros_like(qacc)
    for copy in small:
        copy.wait()
    scale = scale_ref[...]
    mean = mean_ref[...]
    scaled = probe_ref[...].astype(jnp.float32) * scale
    const = jnp.sum(scaled * mean, axis=1, keepdims=True)
    high = scaled.astype(jnp.bfloat16).astype(jnp.float32)
    both = jnp.concatenate([high, scaled - high], axis=0).astype(jnp.bfloat16)
    for b in range(n):
        weights[b] = both[:, b * w : (b + 1) * w]
        means[b] = mean[:, b * w : (b + 1) * w]
        scales[b] = scale[:, b * w : (b + 1) * w]

    lane = lax.broadcasted_iota(jnp.int32, (1, ci), 1)
    plane = lax.rem(lane, si) // sw
    plane_scale = jnp.where(
        plane < 2, jnp.where(plane == 0, 1.0, 1 / 4), jnp.where(plane == 2, 1 / 16, 1 / 64)
    ).astype(jnp.float32)

    def sketch_chunk(c):
        load(c).wait()
        at = pl.multiple_of(c * cw, 8)
        pieces = []
        for sub in range(SUBS):
            total = jnp.zeros((2 * rank, si), jnp.float32)
            for b in range(n):
                packed = words[pl.ds(at + sub * sw, sw), b * w : (b + 1) * w]
                tile = jnp.concatenate(
                    [
                        (packed & (3 << (2 * k))).astype(jnp.float32).astype(jnp.bfloat16)
                        for k in range(PLANES)
                    ],
                    axis=0,
                )
                codes[b, pl.ds(pl.multiple_of(c * ci + sub * si, 16), si), :] = tile
                total += dot_nt(weights[b], tile)
            pieces.append(total)
        total = jnp.concatenate(pieces, axis=1)
        return (total[:rank] + total[rank:]) * plane_scale - const

    def core_copy(c):
        return pltpu.make_async_remote_copy(
            src_ref=sk.at[c], dst_ref=rx_core.at[c], send_sem=core_send.at[c],
            recv_sem=core_recv.at[c], device_id=(ind, other), device_id_type=MESH,
        )

    def y_copy(k, c, slot):
        return pltpu.make_async_remote_copy(
            src_ref=ry.at[y, c], dst_ref=ry.at[slot, c],
            send_sem=y_send.at[k, c], recv_sem=y_recv.at[slot, c],
            device_id=(ind, lax.rem(y + k, ny) * CORES + core), device_id_type=MESH,
        )

    def chunk(c, carry):
        sk[c] = sketch_chunk(c)

        @pl.when(c == 0)
        def _():
            pl.semaphore_wait(barrier, n - 1 + 1 + ny - 1)

        @pl.when(c < CHUNKS)
        def _():
            core_copy(c).start()

        @pl.when(c >= CHUNKS)
        def _():
            j = c - CHUNKS
            core_copy(j).wait_recv()
            ry[y, j] = fold(sk[c] + rx_core[j]).astype(jnp.bfloat16)
            for k in range(1, ny):
                y_copy(k, j, y).start()

        return carry

    lax.fori_loop(0, 2 * CHUNKS, chunk, 0)

    def s_copy(c):
        return pltpu.make_async_remote_copy(
            src_ref=s_out.at[c], dst_ref=s_in.at[c], send_sem=s_send.at[c], recv_sem=s_recv.at[c],
            device_id=(ind, other), device_id_type=MESH,
        )

    def g_copy(k, slot):
        return pltpu.make_async_remote_copy(
            src_ref=rg.at[ind], dst_ref=rg.at[slot],
            send_sem=g_send.at[k], recv_sem=g_recv.at[slot],
            device_id=(lax.rem(ind + k, n), snp), device_id_type=MESH,
        )

    def g_start(k, carry):
        g_copy(k, ind).start()
        return carry

    span = CHUNKS * ci

    def own_half(c, carry):
        gram, row_sum = carry
        for k in range(1, ny):
            y_copy(k, c, lax.rem(y + k, ny)).wait_recv()
        total = ry[0, c].astype(jnp.float32)
        for k in range(1, ny):
            total += ry[k, c].astype(jnp.float32)
        rounded = total.astype(jnp.bfloat16)
        s_out[c] = rounded
        s_copy(c).start()
        piece = unfold(rounded.astype(jnp.float32))
        row_sum = row_sum + jnp.sum(piece, axis=1, keepdims=True)
        exact = piece.astype(jnp.bfloat16)
        gram = gram + dot_nt(exact, exact)
        piece = (piece * plane_scale).astype(jnp.bfloat16)
        at = pl.multiple_of(span + c * ci, 16)
        for b in range(n):
            qacc[b] += jnp.dot(
                piece, codes[b, pl.ds(at, ci), :], preferred_element_type=jnp.float32
            )
        return gram, row_sum

    gram, row_sum = lax.fori_loop(
        0, CHUNKS, own_half,
        (jnp.zeros((rank, rank), jnp.float32), jnp.zeros((rank, 1), jnp.float32)),
    )
    theirs = []
    for c in range(CHUNKS):
        s_copy(c).wait_recv()
        theirs.append(unfold(s_in[c].astype(jnp.float32)))
    theirs = jnp.concatenate(theirs, axis=1)
    row_sum = row_sum + jnp.sum(theirs, axis=1, keepdims=True)
    exact = theirs.astype(jnp.bfloat16)
    gram = gram + dot_nt(exact, exact)
    pad = jnp.zeros((8, 32 - rank), jnp.float32)
    parts = []
    for g in range(rank // 8):
        parts += [gram[8 * g : 8 * g + 8, :], pad]
    parts.append(jnp.zeros((8, 128 - 4 * rank), jnp.float32))
    rg[ind] = jnp.concatenate(parts, axis=1)
    lax.fori_loop(1, n, g_start, 0)
    s_cat[...] = (theirs * jnp.concatenate([plane_scale] * CHUNKS, axis=1)).astype(jnp.bfloat16)

    def rs_copy(k, slot):
        to = lax.rem(ind + k, n)
        return pltpu.make_async_remote_copy(
            src_ref=rs_out.at[to], dst_ref=rs_in.at[slot],
            send_sem=rs_send.at[k], recv_sem=rs_recv.at[slot],
            device_id=(to, snp), device_id_type=MESH,
        )

    def product(k, carry):
        b = lax.rem(ind + k, n)
        q = qacc[b] + jnp.dot(
            s_cat[...], codes[b, 0:span, :], preferred_element_type=jnp.float32
        )
        rs_out[b] = fold(scales[b] * (q - means[b] * row_sum)).astype(jnp.bfloat16)

        @pl.when(k < n)
        def _():
            rs_copy(k, ind).start()

        return carry

    lax.fori_loop(1, n + 1, product, 0)
    rs_in[ind] = rs_out[ind]

    def g_wait(k, carry):
        g_copy(k, lax.rem(ind + k, n)).wait_recv()
        return carry

    lax.fori_loop(1, n, g_wait, 0)
    packed = lax.fori_loop(1, n, lambda k, t: t + rg[k], rg[0])
    lower_inv = inverse_factor(packed, rank)

    def rs_wait(k, carry):
        rs_copy(k, lax.rem(ind + k, n)).wait_recv()
        return carry

    lax.fori_loop(1, n, rs_wait, 0)
    q = lax.fori_loop(
        1, n, lambda k, t: t + rs_in[k].astype(jnp.float32), rs_in[0].astype(jnp.float32)
    )
    loadings = jnp.dot(
        lower_inv, unfold(q), precision=lax.Precision.HIGHEST,
        preferred_element_type=jnp.float32,
    )
    ag[ind] = fold(loadings).astype(jnp.bfloat16)

    def ag_copy(k, slot):
        return pltpu.make_async_remote_copy(
            src_ref=ag.at[ind], dst_ref=ag.at[slot],
            send_sem=ag_send.at[k], recv_sem=ag_recv.at[slot],
            device_id=(lax.rem(ind + k, n), snp), device_id_type=MESH,
        )

    def ag_start(k, carry):
        ag_copy(k, ind).start()
        return carry

    lax.fori_loop(1, n, ag_start, 0)

    def drain(k, carry):
        rs_copy(k, ind).wait_send()
        g_copy(k, ind).wait_send()
        return carry

    lax.fori_loop(1, n, drain, 0)
    for c in range(CHUNKS):
        core_copy(c).wait_send()
        s_copy(c).wait_send()
        for k in range(1, ny):
            y_copy(k, c, y).wait_send()

    for b in range(n):
        @pl.when(ind != b)
        def _():
            ag_copy(1, b).wait_recv()

        out_ref[:, b * w : (b + 1) * w] = unfold(ag[b].astype(jnp.float32)).astype(jnp.bfloat16)

    def drain_ag(k, carry):
        ag_copy(k, ind).wait_send()
        return carry

    lax.fori_loop(1, n, drain_ag, 0)


def on_device(n, ny, genotype, probe, allele_mean, allele_scale):
    word_rows, cols = genotype.shape
    rank = probe.shape[0]
    w = cols // n
    ci = word_rows // (2 * CHUNKS) * PLANES
    f32, b16 = jnp.float32, jnp.bfloat16
    dma = pltpu.SemaphoreType.DMA
    vmem = pl.BlockSpec(memory_space=pltpu.VMEM)
    operands = genotype, probe, allele_mean.reshape(1, cols), allele_scale.reshape(1, cols)
    return pl.pallas_call(
        functools.partial(kernel, n, ny),
        out_shape=jax.ShapeDtypeStruct((rank, cols), b16),
        in_specs=[pl.BlockSpec(memory_space=pltpu.HBM)] * 4,
        out_specs=vmem,
        scratch_shapes=[
            pltpu.VMEM((word_rows, cols), jnp.int32),
            pltpu.VMEM((rank, cols), b16),
            pltpu.VMEM((1, cols), f32),
            pltpu.VMEM((1, cols), f32),
            pltpu.VMEM((n, PLANES * word_rows, w), b16),
            pltpu.VMEM((n, 2 * rank, w), b16),
            pltpu.VMEM((n, 1, w), f32),
            pltpu.VMEM((n, 1, w), f32),
            pltpu.VMEM((2 * CHUNKS, rank, ci), f32),
            pltpu.VMEM((CHUNKS, rank, ci), f32),
            pltpu.VMEM((ny, CHUNKS, 2 * rank, ci // 2), b16),
            pltpu.VMEM((CHUNKS, 2 * rank, ci // 2), b16),
            pltpu.VMEM((CHUNKS, 2 * rank, ci // 2), b16),
            pltpu.VMEM((rank, CHUNKS * ci), b16),
            pltpu.VMEM((n, 8, 128), f32),
            pltpu.VMEM((n, rank, w), f32),
            pltpu.VMEM((n, 2 * rank, w // 2), b16),
            pltpu.VMEM((n, 2 * rank, w // 2), b16),
            pltpu.VMEM((n, 2 * rank, w // 2), b16),
            dma((2 * CHUNKS,)),
            dma((3,)),
            dma((CHUNKS,)), dma((CHUNKS,)),
            dma((ny, CHUNKS)), dma((ny, CHUNKS)),
            dma((CHUNKS,)), dma((CHUNKS,)),
            dma((n,)), dma((n,)),
            dma((n,)), dma((n,)),
            dma((n,)), dma((n,)),
        ],
        compiler_params=pltpu.CompilerParams(
            collective_id=0, has_side_effects=True, vmem_limit_bytes=48 * 1024 * 1024
        ),
        cost_estimate=pl.CostEstimate(
            flops=4 * rank * PLANES * word_rows * cols,
            bytes_accessed=4 * word_rows * cols,
            transcendentals=0,
        ),
    )(*[pltpu.with_memory_space_constraint(x, pltpu.HBM) for x in operands]).astype(f32)


def solution(mesh):
    n = mesh.shape["ind"]
    ny = mesh.shape["snp"] // CORES
    return jax.shard_map(
        functools.partial(on_device, n, ny),
        mesh=mesh,
        in_specs=(P("ind", "snp"), P(None, "snp"), P("snp"), P("snp")),
        out_specs=P(None, "snp"),
        check_vma=False,
    )
```
